128 devices in a mesh: lat: 32 (over y, x_lo, z), mem: 4 (over x_hi, core).
Axes of the slice: x: 4 (x_hi: 2, x_lo: 2; x = x_hi * 2 + x_lo), y: 4, z: 4, core: 2. Of those that a mesh axis runs over, the one named last changes fastest.
Arguments:
- fields: bfloat16 [4, 64, 1440, 256], P('mem', 'lat'), may hold values from -6 to 6
- norm_gain: float32 [256], replicated, may hold values from 0.25 to 1.75
- w_query: bfloat16 [3, 256, 256], replicated, may hold values from -2 to 2
- w_key: bfloat16 [3, 256, 256], replicated, may hold values from -2 to 2
- w_value: bfloat16 [3, 256, 256], replicated, may hold values from -2 to 2
- w_out: bfloat16 [3, 256, 256], replicated, may hold values from -0.375 to 0.375
Outputs:
- mixed: bfloat16 [4, 64, 1440, 256], P('mem', 'lat')
The draws below stay inside these ranges and needn't reach their ends.
All inputs are finite; a program needn't handle non-finite values.
Results may differ from the reference program's by a relative error of at most 0.0086.
Values may be sent and summed in bfloat16 or wider, within the bound.
No kernel may reach another device: no remote copies, remote signals or barrier semaphores. Data moves between devices by JAX's collectives and lax.ppermute only.
A program may use at most 128 MiB of HBM per device.

```python
import math
import jax
import jax.numpy as jnp
from jax import lax

D = 256
HEADS = 8
LON = 1440
LAT = 64
MEMBERS = 4


def key_core(key):
    return jax.random.normal(jax.random.fold_in(key, 101), (3, D, D), jnp.float32)


def head_order(key):
    source = jax.random.fold_in(key, 103)
    orders = [jax.random.permutation(jax.random.fold_in(source, branch), HEADS) for branch in range(3)]
    return jnp.stack(orders).astype(jnp.int32)


def column_values(per_head):
    return jnp.repeat(per_head, D // HEADS, axis=-1)[:, None, :]


def head_scales(key):
    order = head_order(key).astype(jnp.float32)
    rise = jnp.sqrt(order / (HEADS - 1))
    jitter = jax.random.uniform(jax.random.fold_in(key, 104), (3, HEADS), jnp.float32, 0.92, 1.08)
    return (1.2 + 2.3 * rise) * jitter


def draw_w_query(key, part):
    scales = head_scales(key)
    key = jax.random.fold_in(key, 1)
    own = jax.random.normal(key, (3, D, D), jnp.float32)
    weight = column_values(scales) * own / math.sqrt(D)
    return jnp.clip(weight, -2.0, 2.0).astype(jnp.bfloat16)


def draw_w_key(key, part):
    core = key_core(key)
    weight = core / math.sqrt(D)
    return jnp.clip(weight, -2.0, 2.0).astype(jnp.bfloat16)


def draw_w_value(key, part):
    core = key_core(key)
    key = jax.random.fold_in(key, 3)
    noise = jax.random.normal(key, (3, D, D), jnp.float32)
    weight = (1.2 * core + 0.5 * noise) / math.sqrt(D)
    return jnp.clip(weight, -2.0, 2.0).astype(jnp.bfloat16)


def levels(key, extent, pieces, smallest, top_value):
    factor_of, own = 1.0, jax.random.fold_in(key, 6)
    for axis_at, shards_of in pieces:
        draws = jnp.exp(jax.random.uniform(jax.random.fold_in(own, axis_at), (shards_of,), jnp.float32, smallest / len(pieces), top_value / len(pieces)))
        factor_of = factor_of * jnp.repeat(draws, extent[axis_at] // shards_of).reshape([-1 if axis == axis_at else 1 for axis in range(len(extent))])
    return factor_of


def bell_draw(stream_key, shape, scale, limit, cuts=(), held_as=jnp.bfloat16):
    array = scale * jax.random.normal(stream_key, shape, jnp.float32)
    if cuts:
        array = array * levels(stream_key, shape, cuts, -0.22, 0.18)
    return jnp.clip(array, -limit, limit).astype(held_as)


def setup_inputs(seed: int = 0) -> dict:
    arg_keys = jax.random.split(jax.random.key(seed), 7)
    return {
        "fields": bell_draw(arg_keys[0], (MEMBERS, LAT, LON, D), 1.0, 6.0, ((0, 4), (1, 32))),
        "norm_gain": jnp.clip(1.0 + 0.15 * jax.random.normal(arg_keys[1], (D,), jnp.float32), 0.25, 1.75),
        "w_query": draw_w_query(jax.random.fold_in(arg_keys[6], 71), 0),
        "w_key": draw_w_key(jax.random.fold_in(arg_keys[6], 71), 0),
        "w_value": draw_w_value(jax.random.fold_in(arg_keys[6], 71), 0),
        "w_out": bell_draw(arg_keys[5], (3, D, D), D ** -0.5, 0.375),
    }


EPSILON = 1e-06

def rms_normed(fields, norm_gain):
    wide = fields.astype(jnp.float32)
    meansq = lax.optimization_barrier(jnp.mean(wide * wide, axis=-1, keepdims=True))
    return (wide * lax.rsqrt(meansq + EPSILON) * norm_gain.astype(jnp.float32)).astype(jnp.bfloat16)

def project(normed, weight):
    flat = normed.reshape(-1, normed.shape[-1])
    return jnp.dot(flat, weight, preferred_element_type=jnp.float32).astype(jnp.bfloat16).reshape(normed.shape)

def attend_sequence(queries, key_side, value_side):
    lead = queries.shape[:-2]
    length = queries.shape[-2]
    width = queries.shape[-1]
    headsize = width // HEADS
    shape = lead + (length, HEADS, headsize)
    qheads = queries.astype(jnp.float32).reshape(shape)
    kheads = key_side.astype(jnp.float32).reshape(shape)
    vheads = value_side.astype(jnp.float32).reshape(shape)
    scores = jnp.einsum('...she,...the->...hst', qheads, kheads) * (1.0 / math.sqrt(headsize))
    weights = jax.nn.softmax(scores, axis=-1).astype(jnp.bfloat16)
    weights = lax.optimization_barrier(weights).astype(jnp.float32)
    result = jnp.einsum('...hst,...the->...she', weights, vheads)
    return result.reshape(lead + (length, width)).astype(jnp.bfloat16)

def reference(fields, norm_gain, w_query, w_key, w_value, w_out):
    normed = rms_normed(fields, norm_gain)

    def branch_inputs(branch):
        return (project(normed, w_query[branch]), project(normed, w_key[branch]), project(normed, w_value[branch]))
    queries, key_side, value_side = branch_inputs(0)
    rowcount = MEMBERS * LAT
    lon_heads = lax.map(lambda trio: attend_sequence(trio[0], trio[1], trio[2]), (queries.reshape(rowcount, LON, D), key_side.reshape(rowcount, LON, D), value_side.reshape(rowcount, LON, D))).reshape(fields.shape)
    queries, key_side, value_side = branch_inputs(1)
    lat_heads = lax.map(lambda trio: attend_sequence(trio[0], trio[1], trio[2]), (queries.transpose(0, 2, 1, 3), key_side.transpose(0, 2, 1, 3), value_side.transpose(0, 2, 1, 3))).transpose(0, 2, 1, 3)
    queries, key_side, value_side = branch_inputs(2)
    mem_heads = lax.map(lambda trio: attend_sequence(trio[0], trio[1], trio[2]), (queries.transpose(1, 2, 0, 3), key_side.transpose(1, 2, 0, 3), value_side.transpose(1, 2, 0, 3))).transpose(2, 0, 1, 3)
    total = fields.astype(jnp.float32).reshape(-1, D)
    total = total + jnp.dot(lon_heads.reshape(-1, D), w_out[0], preferred_element_type=jnp.float32)
    total = total + jnp.dot(lat_heads.reshape(-1, D), w_out[1], preferred_element_type=jnp.float32)
    total = total + jnp.dot(mem_heads.reshape(-1, D), w_out[2], preferred_element_type=jnp.float32)
    return total.reshape(fields.shape).astype(jnp.bfloat16)
```

```python
import functools
import math

import jax
import jax.numpy as jnp
from jax import lax
from jax.experimental import pallas as pl
from jax.experimental.pallas import tpu as pltpu
from jax.sharding import PartitionSpec as P

HEADS = 8
HEAD = 32
D = 256
EPSILON = 1e-06
QUERY_FACTOR = math.log2(math.e) / math.sqrt(HEAD)
LOW, HIGH = 2.0**-100, 2.0**120
NT = (((1,), (1,)), ((), ()))
MIB = 2**20
WIDE, NARROW = 8, 4
PER = WIDE + NARROW

f32, bf16 = jnp.float32, jnp.bfloat16


def rms_normed(fields, gain):
    wide = fields.astype(f32)
    meansq = jnp.mean(wide * wide, axis=-1, keepdims=True)
    return wide * lax.rsqrt(meansq + EPSILON) * gain


def dot(a, b):
    return jnp.dot(a, b, preferred_element_type=f32)


def pack_kernel(f_ref, g_ref, o_ref, *, parts):
    lon = f_ref.shape[1]
    cut = parts * WIDE
    rest = (lon - cut) // NARROW
    gain = g_ref[...]
    first = [rms_normed(f_ref[r, 0:cut, :], gain).reshape(parts, WIDE, D) for r in range(2)]
    o_ref[:, 0:16, :] = jnp.concatenate(first, axis=1).astype(bf16)
    a, b = [rms_normed(f_ref[r, cut:lon, :], gain).reshape(rest // 2, 8, D) for r in range(2)]
    upper = lax.broadcasted_iota(jnp.int32, a.shape, 1) < 4
    even = jnp.where(upper, a, pltpu.roll(b, 4, 1))
    odd = jnp.where(upper, pltpu.roll(a, 4, 1), b)
    both = jnp.stack([even, odd], axis=1).reshape(rest, 8, D)
    o_ref[0:rest, 16:24, :] = both.astype(bf16)
    o_ref[rest:parts, 16:24, :] = jnp.zeros((parts - rest, 8, D), bf16)


def pack(fields, gain, parts):
    return pl.pallas_call(
        functools.partial(pack_kernel, parts=parts),
        out_shape=jax.ShapeDtypeStruct((parts, 2 * PER, D), bf16),
        compiler_params=pltpu.CompilerParams(vmem_limit_bytes=32 * MIB),
        cost_estimate=pl.CostEstimate(flops=4_000_000, bytes_accessed=3_000_000, transcendentals=0),
        name="pack",
    )(fields, gain)


def unpack_kernel(p0_ref, p1_ref, x_ref, o_ref, *, parts):
    lon = o_ref.shape[1]
    cut = parts * WIDE
    rest = (lon - cut) // NARROW
    partial = (p0_ref, p1_ref)
    first = x_ref[:, 0:16, :].astype(f32)
    for r in range(2):
        add = first[:, 8 * r : 8 * r + 8, :].reshape(cut, D)
        o_ref[r, 0:cut, :] = (partial[r][0:cut, :] + add).astype(bf16)
    both = x_ref[0:rest, 16:24, :].astype(f32).reshape(rest // 2, 2, 8, D)
    even, odd = both[:, 0], both[:, 1]
    upper = lax.broadcasted_iota(jnp.int32, even.shape, 1) < 4
    rows = (jnp.where(upper, even, pltpu.roll(odd, 4, 1)), jnp.where(upper, pltpu.roll(even, 4, 1), odd))
    for r in range(2):
        o_ref[r, cut:lon, :] = (partial[r][cut:lon, :] + rows[r].reshape(lon - cut, D)).astype(bf16)


def unpack(part0, part1, returned):
    parts = returned.shape[0]
    lon = part0.shape[0]
    return pl.pallas_call(
        functools.partial(unpack_kernel, parts=parts),
        out_shape=jax.ShapeDtypeStruct((2, lon, D), bf16),
        compiler_params=pltpu.CompilerParams(vmem_limit_bytes=32 * MIB),
        cost_estimate=pl.CostEstimate(flops=4_000_000, bytes_accessed=6_000_000, transcendentals=0),
        name="unpack",
    )(part0, part1, returned)


def lon_kernel(f_ref, g_ref, wq_ref, wk_ref, wv_ref, wo_ref, o_ref, q_s, kt_s, v_s, acc_s, *, block):
    lon = f_ref.shape[0]
    normed = rms_normed(f_ref[...], g_ref[...]).astype(bf16)
    q_s[...] = (dot(normed, wq_ref[...]) * QUERY_FACTOR).astype(bf16)
    v_s[...] = dot(normed, wv_ref[...]).astype(bf16)
    kt_s[...] = lax.dot_general(wk_ref[...].T, normed, NT, preferred_element_type=f32).astype(bf16)
    row = lax.broadcasted_iota(jnp.int32, (128, lon), 0) // HEAD
    lane = lax.broadcasted_iota(jnp.int32, (lon, 128), 1) // HEAD

    def attend(shifted):
        acc_s[...] = jnp.zeros_like(acc_s)

        @pl.loop(0, HEADS)
        def _(head):
            half = head // 4
            at = pl.multiple_of(half * 128, 128)
            keys = kt_s[pl.ds(at, 128), :]
            keys = jnp.where(row == head % 4, keys, jnp.zeros_like(keys))
            own = lane == head % 4
            values = v_s[:, pl.ds(at, 128)]
            ones = jnp.where(own, 1.0, 0.0).astype(bf16)
            values = jnp.concatenate([jnp.where(own, values, jnp.zeros_like(values)), ones], axis=1)
            for start in range(0, lon, block):
                scores = dot(q_s[start : start + block, pl.ds(at, 128)], keys)
                if shifted:
                    scores = scores - jnp.max(scores, axis=1, keepdims=True)
                weights = jnp.exp2(scores).astype(bf16)
                acc_s[half, start : start + block, :] += dot(weights, values)

    attend(False)
    total = acc_s[:, :, 128:256]
    fine = (jnp.min(total) > LOW) & (jnp.max(total) < HIGH)

    @pl.when(jnp.logical_not(fine))
    def _():
        attend(True)

    heads = [(acc_s[i, :, 0:128] / acc_s[i, :, 128:256]).astype(bf16) for i in range(2)]
    o_ref[...] = f_ref[...].astype(f32) + dot(jnp.concatenate(heads, axis=1), wo_ref[...])


def lon_row(row, gain, w_query, w_key, w_value, w_out):
    lon = row.shape[0]
    return pl.pallas_call(
        functools.partial(lon_kernel, block=lon // 3),
        out_shape=jax.ShapeDtypeStruct((lon, D), f32),
        scratch_shapes=[
            pltpu.VMEM((lon, D), bf16),
            pltpu.VMEM((D, lon), bf16),
            pltpu.VMEM((lon, D), bf16),
            pltpu.VMEM((2, lon, D), f32),
        ],
        compiler_params=pltpu.CompilerParams(vmem_limit_bytes=48 * MIB),
        cost_estimate=pl.CostEstimate(flops=25_000_000_000, bytes_accessed=3_000_000, transcendentals=0),
        name="lon",
    )(row, gain, w_query, w_key, w_value, w_out)


def cross_kernel(x_ref, wq_ref, wk_ref, wv_ref, wo_ref, o_ref, flat_s, x_s, q_s, k_s, v_s, h_s, t_s, *, members):
    parts = x_ref.shape[0]
    groups = parts // members
    seq = 2 * groups
    rows = parts * 2 * PER
    stride = members * 2 * PER

    def place(member, j, r):
        inside = r * WIDE + j if j < WIDE else 2 * WIDE + r * NARROW + (j - WIDE)
        return member * 2 * PER + inside

    wide = x_ref[...].astype(f32).reshape(rows, D)
    flat_s[0] = wide[:, 0:128]
    flat_s[1] = wide[:, 128:256]
    for member in range(members):
        for j in range(PER):
            base = (member * PER + j) * seq
            for c in range(2):
                pieces = [flat_s[c, pl.ds(place(member, j, r), groups, stride=stride), :] for r in range(2)]
                x_s[base : base + seq, 128 * c : 128 * c + 128] = jnp.concatenate(pieces, axis=0).astype(bf16)
    for b in range(2):
        x = x_s[...]
        q_s[b] = (dot(x, wq_ref[b]) * QUERY_FACTOR).astype(bf16)
        k_s[b] = dot(x, wk_ref[b]).astype(bf16)
        v_s[b] = dot(x, wv_ref[b]).astype(bf16)

    head_row = lax.broadcasted_iota(jnp.int32, (4 * seq, 128), 0) // seq
    head_lane = lax.broadcasted_iota(jnp.int32, (4 * seq, 128), 1) // HEAD
    own = head_row == head_lane
    ones = jnp.where(own, 1.0, 0.0).astype(bf16)

    def lat_attend(shifted):
        @pl.loop(0, members * PER // 4)
        def _(n):
            for u in range(4):
                at = pl.multiple_of((n * 4 + u) * seq, seq)
                for c in range(2):
                    lanes = slice(128 * c, 128 * c + 128)
                    keys = jnp.concatenate([k_s[0, pl.ds(at, seq), lanes]] * 4, axis=0)
                    keys = jnp.where(own, keys, jnp.zeros_like(keys))
                    values = jnp.concatenate([v_s[0, pl.ds(at, seq), lanes]] * 4, axis=0)
                    values = jnp.where(own, values, jnp.zeros_like(values))
                    scores = lax.dot_general(
                        q_s[0, pl.ds(at, seq), lanes], keys, NT, preferred_element_type=f32
                    )
                    if shifted:
                        of = lax.broadcasted_iota(jnp.int32, scores.shape, 1) // seq
                        for h in range(4):
                            top = jnp.max(jnp.where(of == h, scores, -jnp.inf), axis=1, keepdims=True)
                            scores = jnp.where(of == h, scores - top, scores)
                    weights = jnp.exp2(scores).astype(bf16)
                    total = dot(weights, ones)
                    h_s[pl.ds(at, seq), lanes] = (dot(weights, values) / total).astype(bf16)
                    t_s[pl.ds(at, seq), lanes] = total

    lat_attend(False)
    fine = (jnp.min(t_s[...]) > LOW) & (jnp.max(t_s[...]) < HIGH)

    @pl.when(jnp.logical_not(fine))
    def _():
        lat_attend(True)

    block = jnp.where(
        lax.broadcasted_iota(jnp.int32, (D, D), 0) // HEAD == lax.broadcasted_iota(jnp.int32, (D, D), 1) // HEAD,
        1.0,
        0.0,
    ).astype(bf16)

    @pl.loop(0, PER)
    def _(j):
        ats = [pl.multiple_of((member * PER + j) * seq, seq) for member in range(members)]
        keys = [k_s[1, pl.ds(at, seq), :] for at in ats]
        values = [v_s[1, pl.ds(at, seq), :].astype(f32) for at in ats]
        for at in ats:
            query = q_s[1, pl.ds(at, seq), :]
            scores = dot(jnp.concatenate([query * key for key in keys], axis=0), block)
            scores = [scores[i * seq : i * seq + seq] for i in range(members)]
            top = functools.reduce(jnp.maximum, scores)
            weights = [jnp.exp2(s - top) for s in scores]
            total = functools.reduce(jnp.add, weights)
            mixed = functools.reduce(jnp.add, [w * v for w, v in zip(weights, values)])
            h_s[pl.ds(at, seq), D : 2 * D] = (mixed / total).astype(bf16)

    out = dot(h_s[...], wo_ref[...])
    for member in range(members):
        for j in range(PER):
            base = (member * PER + j) * seq
            for c in range(2):
                for r in range(2):
                    piece = out[base + r * groups : base + (r + 1) * groups, 128 * c : 128 * c + 128]
                    flat_s[c, pl.ds(place(member, j, r), groups, stride=stride), :] = piece
    o_ref[...] = jnp.concatenate([flat_s[0], flat_s[1]], axis=1).reshape(parts, 2 * PER, D).astype(bf16)


def cross(received, w_query, w_key, w_value, w_out, members):
    parts = received.shape[0]
    rows = parts * 2 * PER
    return pl.pallas_call(
        functools.partial(cross_kernel, members=members),
        out_shape=jax.ShapeDtypeStruct(received.shape, bf16),
        scratch_shapes=[
            pltpu.VMEM((2, rows, 128), f32),
            pltpu.VMEM((rows, D), bf16),
            pltpu.VMEM((2, rows, D), bf16),
            pltpu.VMEM((2, rows, D), bf16),
            pltpu.VMEM((2, rows, D), bf16),
            pltpu.VMEM((rows, 2 * D), bf16),
            pltpu.VMEM((rows, D), f32),
        ],
        compiler_params=pltpu.CompilerParams(vmem_limit_bytes=56 * MIB),
        cost_estimate=pl.CostEstimate(flops=12_000_000_000, bytes_accessed=5_000_000, transcendentals=0),
        name="cross",
    )(received, w_query, w_key, w_value, w_out)


def on_device(fields, norm_gain, w_query, w_key, w_value, w_out, *, lat, members):
    state = fields.reshape(fields.shape[1:])
    gain = norm_gain.reshape(1, D)
    axes = ("lat", "mem")
    packed = pack(state, gain, lat * members)
    received = lax.all_to_all(packed, axes, split_axis=0, concat_axis=0, tiled=True)
    part0 = lon_row(state[0], gain, w_query[0], w_key[0], w_value[0], w_out[0])
    received, part0 = lax.optimization_barrier((received, part0))
    sent = cross(received, w_query[1:], w_key[1:], w_value[1:], w_out[1:].reshape(2 * D, D), members)
    returned = lax.all_to_all(sent, axes, split_axis=0, concat_axis=0, tiled=True)
    row1, sent = lax.optimization_barrier((state[1], sent))
    part1 = lon_row(row1, gain, w_query[0], w_key[0], w_value[0], w_out[0])
    return unpack(part0, part1, returned).reshape(fields.shape)


def solution(mesh):
    return jax.shard_map(
        functools.partial(on_device, lat=mesh.shape["lat"], members=mesh.shape["mem"]),
        mesh=mesh,
        in_specs=(P("mem", "lat", None, None), P(), P(), P(), P(), P()),
        out_specs=P("mem", "lat", None, None),
        check_vma=False,
    )
```

```python
import functools
import math

import jax
import jax.numpy as jnp
from jax import lax
from jax.experimental import pallas as pl
from jax.experimental.pallas import tpu as pltpu
from jax.sharding import PartitionSpec as P

HEADS = 8
HEAD = 32
D = 256
EPSILON = 1e-06
QUERY_FACTOR = math.log2(math.e) / math.sqrt(HEAD)
LOW, HIGH = 2.0**-100, 2.0**120
NT = (((1,), (1,)), ((), ()))
MIB = 2**20
WIDE, NARROW = 8, 4
PER = WIDE + NARROW
STEPS = 4

f32, bf16 = jnp.float32, jnp.bfloat16


def rms_normed(fields, gain):
    wide = fields.astype(f32)
    meansq = jnp.mean(wide * wide, axis=-1, keepdims=True)
    return wide * lax.rsqrt(meansq + EPSILON) * gain


def dot(a, b):
    return jnp.dot(a, b, preferred_element_type=f32)


ANY = pl.BlockSpec(memory_space=pl.ANY)


def start_all(copies):
    for copy in copies:
        copy.start()
    return copies


def spans(step, parts, lon):
    count = parts // STEPS
    cut = parts * WIDE
    narrow = cut + step * count * NARROW
    return (
        (step * count, count),
        (step * count * WIDE, count * WIDE),
        (narrow, max(0, min(count * NARROW, lon - narrow))),
    )


def pack_kernel(f_hbm, g_hbm, o_ref, f_s, g_s, sem, g_sem, *, parts):
    lon = f_hbm.shape[1]
    all_spans = [spans(step, parts, lon) for step in range(STEPS)]
    gain_copy = pltpu.make_async_copy(g_hbm, g_s, g_sem)
    gain_copy.start()
    copies = [
        start_all(
            [
                pltpu.make_async_copy(f_hbm.at[:, pl.ds(at, n)], f_s.at[:, pl.ds(at, n)], sem.at[step, i])
                for i, (at, n) in enumerate(all_spans[step][1:])
                if n
            ]
        )
        for step in range(STEPS)
    ]
    gain_copy.wait()
    gain = g_s[...]
    for step, ((dev, count), (at, n), (at2, n2)) in enumerate(all_spans):
        for copy in copies[step]:
            copy.wait()
        first = [rms_normed(f_s[r, at : at + n, :], gain).reshape(count, WIDE, D) for r in range(2)]
        o_ref[dev : dev + count, 0:16, :] = jnp.concatenate(first, axis=1).astype(bf16)
        have = n2 // NARROW
        if have:
            a, b = [rms_normed(f_s[r, at2 : at2 + n2, :], gain).reshape(have // 2, 8, D) for r in range(2)]
            upper = lax.broadcasted_iota(jnp.int32, a.shape, 1) < 4
            even = jnp.where(upper, a, pltpu.roll(b, 4, 1))
            odd = jnp.where(upper, pltpu.roll(a, 4, 1), b)
            both = jnp.stack([even, odd], axis=1).reshape(have, 8, D)
            o_ref[dev : dev + have, 16:24, :] = both.astype(bf16)
        if have < count:
            o_ref[dev + have : dev + count, 16:24, :] = jnp.zeros((count - have, 8, D), bf16)


def pack(fields, gain, parts):
    return pl.pallas_call(
        functools.partial(pack_kernel, parts=parts),
        out_shape=jax.ShapeDtypeStruct((parts, 2 * PER, D), bf16),
        in_specs=[ANY, ANY],
        scratch_shapes=[
            pltpu.VMEM(fields.shape, bf16),
            pltpu.VMEM((1, D), f32),
            pltpu.SemaphoreType.DMA((STEPS, 2)),
            pltpu.SemaphoreType.DMA,
        ],
        compiler_params=pltpu.CompilerParams(vmem_limit_bytes=16 * MIB),
        cost_estimate=pl.CostEstimate(flops=4_000_000, bytes_accessed=3_000_000, transcendentals=0),
        name="pack",
    )(fields, gain)


def unpack_kernel(p0_hbm, p1_hbm, x_hbm, o_hbm, p_s, x_s, o_s, in_sem, out_sem, *, parts):
    lon = o_hbm.shape[1]
    all_spans = [spans(step, parts, lon) for step in range(STEPS)]
    copies = []
    for step, ((dev, count), *lons) in enumerate(all_spans):
        mine = [pltpu.make_async_copy(x_hbm.at[pl.ds(dev, count)], x_s.at[pl.ds(dev, count)], in_sem.at[step, 4])]
        for i, (at, n) in enumerate(lons):
            for r, p_hbm in enumerate((p0_hbm, p1_hbm)):
                if n:
                    part = p_hbm.at[pl.ds(at, n)]
                    mine.append(pltpu.make_async_copy(part, p_s.at[r, pl.ds(at, n)], in_sem.at[step, 2 * i + r]))
        copies.append(start_all(mine))
    outs = []
    for step, ((dev, count), (at, n), (at2, n2)) in enumerate(all_spans):
        for copy in copies[step]:
            copy.wait()
        first = x_s[dev : dev + count, 0:16, :].astype(f32)
        for r in range(2):
            add = first[:, 8 * r : 8 * r + 8, :].reshape(n, D)
            o_s[r, at : at + n, :] = (p_s[r, at : at + n, :] + add).astype(bf16)
        have = n2 // NARROW
        if have:
            both = x_s[dev : dev + have, 16:24, :].astype(f32).reshape(have // 2, 2, 8, D)
            even, odd = both[:, 0], both[:, 1]
            upper = lax.broadcasted_iota(jnp.int32, even.shape, 1) < 4
            rows = (jnp.where(upper, even, pltpu.roll(odd, 4, 1)), jnp.where(upper, pltpu.roll(even, 4, 1), odd))
            for r in range(2):
                o_s[r, at2 : at2 + n2, :] = (p_s[r, at2 : at2 + n2, :] + rows[r].reshape(n2, D)).astype(bf16)
        for i, (to, m) in enumerate(((at, n), (at2, n2))):
            if m:
                copy = pltpu.make_async_copy(o_s.at[:, pl.ds(to, m)], o_hbm.at[:, pl.ds(to, m)], out_sem.at[step, i])
                copy.start()
                outs.append(copy)
    for copy in outs:
        copy.wait()


def unpack(part0, part1, returned):
    parts = returned.shape[0]
    lon = part0.shape[0]
    return pl.pallas_call(
        functools.partial(unpack_kernel, parts=parts),
        out_shape=jax.ShapeDtypeStruct((2, lon, D), bf16),
        in_specs=[ANY, ANY, ANY],
        out_specs=ANY,
        scratch_shapes=[
            pltpu.VMEM((2, lon, D), f32),
            pltpu.VMEM(returned.shape, bf16),
            pltpu.VMEM((2, lon, D), bf16),
            pltpu.SemaphoreType.DMA((STEPS, 5)),
            pltpu.SemaphoreType.DMA((STEPS, 2)),
        ],
        compiler_params=pltpu.CompilerParams(vmem_limit_bytes=20 * MIB),
        cost_estimate=pl.CostEstimate(flops=4_000_000, bytes_accessed=6_000_000, transcendentals=0),
        name="unpack",
    )(part0, part1, returned)


def out_of_range(total):
    return jnp.where((total > LOW) & (total < HIGH), 0.0, 1.0)


def lon_kernel(after, f_hbm, g_hbm, wq_hbm, wk_hbm, wv_hbm, wo_hbm, o_ref, f_s, g_s, w_s, q_s, kt_s, v_s, acc_s, sem, *, row_at, block):
    del after
    lon = f_s.shape[0]
    copies = [pltpu.make_async_copy(f_hbm.at[row_at], f_s, sem.at[0]), pltpu.make_async_copy(g_hbm, g_s, sem.at[1])]
    for i, w_hbm in enumerate((wk_hbm, wq_hbm, wv_hbm, wo_hbm)):
        copies.append(pltpu.make_async_copy(w_hbm.at[0], w_s.at[i], sem.at[2 + i]))
    start_all(copies)
    copies[0].wait()
    copies[1].wait()
    normed = rms_normed(f_s[...], g_s[...]).astype(bf16)
    copies[2].wait()
    kt_s[...] = lax.dot_general(w_s[0].T, normed, NT, preferred_element_type=f32).astype(bf16)
    copies[3].wait()
    q_s[...] = (dot(normed, w_s[1]) * QUERY_FACTOR).astype(bf16)
    copies[4].wait()
    v_s[...] = dot(normed, w_s[2]).astype(bf16)
    copies[5].wait()
    row = lax.broadcasted_iota(jnp.int32, (128, lon), 0) // HEAD
    lane = lax.broadcasted_iota(jnp.int32, (lon, 128), 1) // HEAD

    def attend(shifted):
        acc_s[...] = jnp.zeros_like(acc_s)

        @pl.loop(0, HEADS)
        def _(head):
            half = head // 4
            at = pl.multiple_of(half * 128, 128)
            keys = kt_s[pl.ds(at, 128), :]
            keys = jnp.where(row == head % 4, keys, jnp.zeros_like(keys))
            own = lane == head % 4
            values = v_s[:, pl.ds(at, 128)]
            ones = jnp.where(own, 1.0, 0.0).astype(bf16)
            values = jnp.concatenate([jnp.where(own, values, jnp.zeros_like(values)), ones], axis=1)

            def score(start):
                scores = dot(q_s[start : start + block, pl.ds(at, 128)], keys)
                if shifted:
                    scores = scores - jnp.max(scores, axis=1, keepdims=True)
                return scores

            ahead = score(0)
            for start in range(0, lon, block):
                weights = jnp.exp2(ahead).astype(bf16)
                if start + block < lon:
                    ahead = score(start + block)
                acc_s[half, start : start + block, :] += dot(weights, values)

    attend(False)
    bad = jnp.max(out_of_range(acc_s[:, :, 128:256]))

    @pl.when(bad > 0.0)
    def _():
        attend(True)

    heads = [(acc_s[i, :, 0:128] / acc_s[i, :, 128:256]).astype(bf16) for i in range(2)]
    o_ref[...] = f_s[...].astype(f32) + dot(jnp.concatenate(heads, axis=1), w_s[3])


def lon_row(after, fields, gain, w_query, w_key, w_value, w_out, row_at):
    lon = fields.shape[1]
    return pl.pallas_call(
        functools.partial(lon_kernel, row_at=row_at, block=lon // 2),
        out_shape=jax.ShapeDtypeStruct((lon, D), f32),
        in_specs=[ANY] * 7,
        scratch_shapes=[
            pltpu.VMEM((lon, D), bf16),
            pltpu.VMEM((1, D), f32),
            pltpu.VMEM((4, D, D), bf16),
            pltpu.VMEM((lon, D), bf16),
            pltpu.VMEM((D, lon), bf16),
            pltpu.VMEM((lon, D), bf16),
            pltpu.VMEM((2, lon, D), f32),
            pltpu.SemaphoreType.DMA((6,)),
        ],
        compiler_params=pltpu.CompilerParams(vmem_limit_bytes=48 * MIB),
        cost_estimate=pl.CostEstimate(flops=25_000_000_000, bytes_accessed=3_000_000, transcendentals=0),
        name="lon",
    )(after, fields, gain, w_query, w_key, w_value, w_out)


def cross_kernel(
    after, x_hbm, wq_hbm, wk_hbm, wv_hbm, wo_hbm, o_hbm,
    in_s, w_s, flat_s, x_s, q_s, k_s, v_s, h_s, bad_s, in_sem, w_sem, out_sem, *, members,
):
    del after
    parts = x_hbm.shape[0]
    groups = parts // members
    seq = 2 * groups
    rows = parts * 2 * PER
    block = members * 2 * PER
    stride = flat_s.shape[1] // groups
    share = parts // STEPS

    loads = [
        pltpu.make_async_copy(x_hbm.at[pl.ds(i * share, share)], in_s.at[pl.ds(i * share, share)], in_sem.at[i])
        for i in range(STEPS)
    ]
    weights_in = []
    for i, w_hbm in enumerate((wq_hbm, wk_hbm, wv_hbm, wo_hbm)):
        weights_in.append(pltpu.make_async_copy(w_hbm.at[pl.ds(1, 2)], w_s.at[i], w_sem.at[i]))
    start_all(loads + weights_in)

    def place(member, j, r):
        inside = r * WIDE + j if j < WIDE else 2 * WIDE + r * NARROW + (j - WIDE)
        return member * 2 * PER + inside

    for i in range(STEPS):
        loads[i].wait()
        for g in range(i * groups // STEPS, (i + 1) * groups // STEPS):
            wide = in_s[g * members : (g + 1) * members].astype(f32).reshape(block, D)
            for c in range(2):
                flat_s[c, g * stride : g * stride + block, :] = wide[:, 128 * c : 128 * c + 128]
    for member in range(members):
        for j in range(PER):
            base = (member * PER + j) * seq
            for c in range(2):
                pieces = [flat_s[c, pl.ds(place(member, j, r), groups, stride=stride), :] for r in range(2)]
                x_s[base : base + seq, 128 * c : 128 * c + 128] = jnp.concatenate(pieces, axis=0).astype(bf16)
    for copy in weights_in:
        copy.wait()

    @pl.loop(0, 3)
    def _(n):
        at = pl.multiple_of(n * (rows // 3), rows // 3)
        x = x_s[pl.ds(at, rows // 3), :]
        for b in range(2):
            q_s[b, pl.ds(at, rows // 3), :] = (dot(x, w_s[0, b]) * QUERY_FACTOR).astype(bf16)
            k_s[b, pl.ds(at, rows // 3), :] = dot(x, w_s[1, b]).astype(bf16)
            v_s[b, pl.ds(at, rows // 3), :] = dot(x, w_s[2, b]).astype(bf16)

    twice = 2 * seq
    own = lax.broadcasted_iota(jnp.int32, (twice, 128), 0) // seq
    own = own == (lax.broadcasted_iota(jnp.int32, (twice, 128), 1) // HEAD) % 2
    ones = jnp.where(own, 1.0, 0.0).astype(bf16)
    left = lax.broadcasted_iota(jnp.int32, (seq, 128), 1) < 64

    def lat_score(spot, shifted):
        at, lanes = spot
        query, key = q_s[0, pl.ds(at, seq), lanes], k_s[0, pl.ds(at, seq), lanes]
        none = jnp.zeros_like(query)
        keys = jnp.concatenate([key, key], axis=0)
        keys = jnp.where(own, keys, jnp.zeros_like(keys))
        queries = jnp.concatenate([jnp.where(left, query, none), jnp.where(left, none, query)], axis=0)
        scores = lax.dot_general(queries, keys, NT, preferred_element_type=f32)
        if shifted:
            first = lax.broadcasted_iota(jnp.int32, scores.shape, 1) < seq
            tops = [jnp.max(jnp.where(first == side, scores, -jnp.inf), axis=1, keepdims=True) for side in (True, False)]
            scores = scores - jnp.where(first, tops[0], tops[1])
        return scores

    def lat_finish(spot, scores):
        at, lanes = spot
        value = v_s[0, pl.ds(at, seq), lanes]
        values = jnp.concatenate([value, value], axis=0)
        values = jnp.where(own, values, jnp.zeros_like(values))
        weights = jnp.exp2(scores).astype(bf16)
        mixed, total = dot(weights, values), dot(weights, ones)
        return jnp.where(left, mixed[:seq], mixed[seq:]), jnp.where(left, total[:seq], total[seq:])

    def lat_attend(shifted, several):
        @pl.loop(0, members * PER // several)
        def _(n):
            spots = [
                (pl.multiple_of((n * several + u) * seq, seq), slice(128 * c, 128 * c + 128))
                for u in range(several)
                for c in range(2)
            ]
            scores = [lat_score(spot, shifted) for spot in spots]
            results = [lat_finish(spot, score) for spot, score in zip(spots, scores)]
            for (at, lanes), (mixed, total) in zip(spots, results):
                h_s[pl.ds(at, seq), lanes] = (mixed / total).astype(bf16)
            if not shifted:
                bad_s[...] = functools.reduce(jnp.maximum, [out_of_range(total) for _, total in results], bad_s[...])

    bad_s[...] = jnp.zeros_like(bad_s)
    lat_attend(False, 8)
    bad = jnp.max(bad_s[...])

    @pl.when(bad > 0.0)
    def _():
        lat_attend(True, 1)

    count = PER * seq
    piece = count // 4
    feature = lax.broadcasted_iota(jnp.int32, (D, 128), 0) // HEAD
    lane = lax.broadcasted_iota(jnp.int32, (D, 128), 1)
    fold = jnp.concatenate(
        [
            jnp.where(lane == n * 32 + m * HEADS + feature, 1.0, 0.0).astype(bf16)
            for m in range(members)
            for n in range(members)
        ],
        axis=0,
    )
    slot = lax.broadcasted_iota(jnp.int32, (128, D), 0)
    feature = lax.broadcasted_iota(jnp.int32, (128, D), 1) // HEAD
    spread = [
        jnp.concatenate(
            [jnp.where(slot == n * 32 + m * HEADS + feature, 1.0, 0.0).astype(bf16) for n in range(members)], axis=1
        )
        for m in range(members)
    ]
    spots = [[i * piece + member * count for member in range(members)] for i in range(4)]

    def over_members(combine, x):
        return functools.reduce(combine, [pltpu.roll(x, 32 * n, 1) for n in (1, 2, 3)], x)

    def mem_weights(ats):
        keys = [k_s[1, at : at + piece, :] for at in ats]
        queries = [q_s[1, at : at + piece, :] for at in ats]
        scores = dot(jnp.concatenate([query * key for query in queries for key in keys], axis=1), fold)
        weights = jnp.exp2(scores - over_members(jnp.maximum, scores))
        return (weights / over_members(jnp.add, weights)).astype(bf16)

    def mem_finish(ats, weights):
        values = [v_s[1, at : at + piece, :].astype(f32) for at in ats]
        for m in range(members):
            wide = dot(weights, spread[m])
            terms = [wide[:, n * D : n * D + D] * values[n] for n in range(members)]
            h_s[ats[m] : ats[m] + piece, D : 2 * D] = functools.reduce(jnp.add, terms).astype(bf16)

    ahead = mem_weights(spots[0])
    for i, ats in enumerate(spots):
        weights = ahead
        if i + 1 < len(spots):
            ahead = mem_weights(spots[i + 1])
        mem_finish(ats, weights)

    for member in range(members):
        base = member * PER * seq
        h = h_s[base : base + PER * seq, :]
        out = dot(h[:, 0:D], w_s[3, 0]) + dot(h[:, D : 2 * D], w_s[3, 1])
        for j in range(PER):
            for c in range(2):
                for r in range(2):
                    at = j * seq + r * groups
                    value = out[at : at + groups, 128 * c : 128 * c + 128]
                    flat_s[c, pl.ds(place(member, j, r), groups, stride=stride), :] = value
    stores = []
    for i in range(STEPS):
        for g in range(i * groups // STEPS, (i + 1) * groups // STEPS):
            both = jnp.concatenate([flat_s[c, g * stride : g * stride + block, :] for c in range(2)], axis=1)
            in_s[g * members : (g + 1) * members] = both.reshape(members, 2 * PER, D).astype(bf16)
        part = pl.ds(i * share, share)
        stores.append(pltpu.make_async_copy(in_s.at[part], o_hbm.at[part], out_sem.at[i]))
        stores[-1].start()
    for copy in stores:
        copy.wait()


def cross(after, received, w_query, w_key, w_value, w_out, members):
    parts = received.shape[0]
    rows = parts * 2 * PER
    groups = parts // members
    return pl.pallas_call(
        functools.partial(cross_kernel, members=members),
        out_shape=jax.ShapeDtypeStruct(received.shape, bf16),
        in_specs=[ANY] * 6,
        out_specs=ANY,
        scratch_shapes=[
            pltpu.VMEM(received.shape, bf16),
            pltpu.VMEM((4, 2, D, D), bf16),
            pltpu.VMEM((2, rows + 8 * groups, 128), f32),
            pltpu.VMEM((rows, D), bf16),
            pltpu.VMEM((2, rows, D), bf16),
            pltpu.VMEM((2, rows, D), bf16),
            pltpu.VMEM((2, rows, D), bf16),
            pltpu.VMEM((rows, 2 * D), bf16),
            pltpu.VMEM((2 * groups, 128), f32),
            pltpu.SemaphoreType.DMA((STEPS,)),
            pltpu.SemaphoreType.DMA((4,)),
            pltpu.SemaphoreType.DMA((STEPS,)),
        ],
        compiler_params=pltpu.CompilerParams(vmem_limit_bytes=56 * MIB),
        cost_estimate=pl.CostEstimate(flops=12_000_000_000, bytes_accessed=5_000_000, transcendentals=0),
        name="cross",
    )(after, received, w_query, w_key, w_value, w_out)


def on_device(fields, norm_gain, w_query, w_key, w_value, w_out, *, lat, members):
    state = fields.reshape(fields.shape[1:])
    gain = norm_gain.reshape(1, D)
    axes = ("lat", "mem")
    weights = (w_query, w_key, w_value, w_out)
    packed = pack(state, gain, lat * members)
    received = lax.all_to_all(packed, axes, split_axis=0, concat_axis=0, tiled=True)
    part0 = lon_row(packed, state, gain, *weights, 0)
    sent = cross(part0, received, *weights, members)
    returned = lax.all_to_all(sent, axes, split_axis=0, concat_axis=0, tiled=True)
    part1 = lon_row(sent, state, gain, *weights, 1)
    return unpack(part0, part1, returned).reshape(fields.shape)


def solution(mesh):
    return jax.shard_map(
        functools.partial(on_device, lat=mesh.shape["lat"], members=mesh.shape["mem"]),
        mesh=mesh,
        in_specs=(P("mem", "lat", None, None), P(), P(), P(), P(), P()),
        out_specs=P("mem", "lat", None, None),
        check_vma=False,
    )
```

```python
import functools
import math

import jax
import jax.numpy as jnp
from jax import lax
from jax.experimental import pallas as pl
from jax.experimental.pallas import tpu as pltpu
from jax.sharding import PartitionSpec as P

HEADS = 8
HEAD = 32
D = 256
EPSILON = 1e-06
QUERY_FACTOR = math.log2(math.e) / math.sqrt(HEAD)
LOW, HIGH = 2.0**-100, 2.0**120
NT = (((1,), (1,)), ((), ()))
MIB = 2**20
WIDE, NARROW = 8, 4
PER = WIDE + NARROW
STEPS = 4
VMEM = 60 * MIB

f32, bf16 = jnp.float32, jnp.bfloat16


def rms_normed(fields, gain):
    wide = fields.astype(f32)
    meansq = jnp.mean(wide * wide, axis=-1, keepdims=True)
    return wide * lax.rsqrt(meansq + EPSILON) * gain


def dot(a, b):
    return jnp.dot(a, b, preferred_element_type=f32)


ANY = pl.BlockSpec(memory_space=pl.ANY)


def start_all(copies):
    for copy in copies:
        copy.start()
    return copies


def spans(step, parts, lon):
    count = parts // STEPS
    cut = parts * WIDE
    narrow = cut + step * count * NARROW
    return (
        (step * count, count),
        (step * count * WIDE, count * WIDE),
        (narrow, max(0, min(count * NARROW, lon - narrow))),
    )


def pack_kernel(f_hbm, g_hbm, o_ref, f_s, g_s, sem, g_sem, *, parts):
    lon = f_hbm.shape[1]
    all_spans = [spans(step, parts, lon) for step in range(STEPS)]
    gain_copy = pltpu.make_async_copy(g_hbm, g_s, g_sem)
    gain_copy.start()
    copies = [
        start_all(
            [
                pltpu.make_async_copy(f_hbm.at[:, pl.ds(at, n)], f_s.at[:, pl.ds(at, n)], sem.at[step, i])
                for i, (at, n) in enumerate(all_spans[step][1:])
                if n
            ]
        )
        for step in range(STEPS)
    ]
    gain_copy.wait()
    gain = g_s[...]
    for step, ((dev, count), (at, n), (at2, n2)) in enumerate(all_spans):
        for copy in copies[step]:
            copy.wait()
        first = [rms_normed(f_s[r, at : at + n, :], gain).reshape(count, WIDE, D) for r in range(2)]
        o_ref[dev : dev + count, 0:16, :] = jnp.concatenate(first, axis=1).astype(bf16)
        have = n2 // NARROW
        if have:
            a, b = [rms_normed(f_s[r, at2 : at2 + n2, :], gain).reshape(have // 2, 8, D) for r in range(2)]
            upper = lax.broadcasted_iota(jnp.int32, a.shape, 1) < 4
            even = jnp.where(upper, a, pltpu.roll(b, 4, 1))
            odd = jnp.where(upper, pltpu.roll(a, 4, 1), b)
            both = jnp.stack([even, odd], axis=1).reshape(have, 8, D)
            o_ref[dev : dev + have, 16:24, :] = both.astype(bf16)
        if have < count:
            o_ref[dev + have : dev + count, 16:24, :] = jnp.zeros((count - have, 8, D), bf16)


def pack(fields, gain, parts):
    return pl.pallas_call(
        functools.partial(pack_kernel, parts=parts),
        out_shape=jax.ShapeDtypeStruct((parts, 2 * PER, D), bf16),
        in_specs=[ANY, ANY],
        scratch_shapes=[
            pltpu.VMEM(fields.shape, bf16),
            pltpu.VMEM((1, D), f32),
            pltpu.SemaphoreType.DMA((STEPS, 2)),
            pltpu.SemaphoreType.DMA,
        ],
        compiler_params=pltpu.CompilerParams(vmem_limit_bytes=VMEM),
        cost_estimate=pl.CostEstimate(flops=4_000_000, bytes_accessed=3_000_000, transcendentals=0),
        name="pack",
    )(fields, gain)


def unpack_kernel(p0_hbm, p1_hbm, x_hbm, o_hbm, p_s, x_s, o_s, in_sem, out_sem, *, parts):
    lon = o_hbm.shape[1]
    all_spans = [spans(step, parts, lon) for step in range(STEPS)]
    copies = []
    for step, ((dev, count), *lons) in enumerate(all_spans):
        mine = [pltpu.make_async_copy(x_hbm.at[pl.ds(dev, count)], x_s.at[pl.ds(dev, count)], in_sem.at[step, 4])]
        for i, (at, n) in enumerate(lons):
            for r, p_hbm in enumerate((p0_hbm, p1_hbm)):
                if n:
                    part = p_hbm.at[pl.ds(at, n)]
                    mine.append(pltpu.make_async_copy(part, p_s.at[r, pl.ds(at, n)], in_sem.at[step, 2 * i + r]))
        copies.append(start_all(mine))
    outs = []
    for step, ((dev, count), (at, n), (at2, n2)) in enumerate(all_spans):
        for copy in copies[step]:
            copy.wait()
        first = x_s[dev : dev + count, 0:16, :].astype(f32)
        for r in range(2):
            add = first[:, 8 * r : 8 * r + 8, :].reshape(n, D)
            o_s[r, at : at + n, :] = (p_s[r, at : at + n, :] + add).astype(bf16)
        have = n2 // NARROW
        if have:
            both = x_s[dev : dev + have, 16:24, :].astype(f32).reshape(have // 2, 2, 8, D)
            even, odd = both[:, 0], both[:, 1]
            upper = lax.broadcasted_iota(jnp.int32, even.shape, 1) < 4
            rows = (jnp.where(upper, even, pltpu.roll(odd, 4, 1)), jnp.where(upper, pltpu.roll(even, 4, 1), odd))
            for r in range(2):
                o_s[r, at2 : at2 + n2, :] = (p_s[r, at2 : at2 + n2, :] + rows[r].reshape(n2, D)).astype(bf16)
        for i, (to, m) in enumerate(((at, n), (at2, n2))):
            if m:
                copy = pltpu.make_async_copy(o_s.at[:, pl.ds(to, m)], o_hbm.at[:, pl.ds(to, m)], out_sem.at[step, i])
                copy.start()
                outs.append(copy)
    for copy in outs:
        copy.wait()


def unpack(part0, part1, returned):
    parts = returned.shape[0]
    lon = part0.shape[0]
    return pl.pallas_call(
        functools.partial(unpack_kernel, parts=parts),
        out_shape=jax.ShapeDtypeStruct((2, lon, D), bf16),
        in_specs=[ANY, ANY, ANY],
        out_specs=ANY,
        scratch_shapes=[
            pltpu.VMEM((2, lon, D), f32),
            pltpu.VMEM(returned.shape, bf16),
            pltpu.VMEM((2, lon, D), bf16),
            pltpu.SemaphoreType.DMA((STEPS, 5)),
            pltpu.SemaphoreType.DMA((STEPS, 2)),
        ],
        compiler_params=pltpu.CompilerParams(vmem_limit_bytes=VMEM),
        cost_estimate=pl.CostEstimate(flops=4_000_000, bytes_accessed=6_000_000, transcendentals=0),
        name="unpack",
    )(part0, part1, returned)


def out_of_range(total):
    return jnp.where((total > LOW) & (total < HIGH), 0.0, 1.0)


def lon_kernel(after, f_hbm, g_hbm, wq_hbm, wk_hbm, wv_hbm, wo_hbm, o_ref, f_s, g_s, w_s, q_s, kt_s, v_s, acc_s, sem, *, row_at, block):
    del after
    lon = f_s.shape[0]
    copies = [pltpu.make_async_copy(f_hbm.at[row_at], f_s, sem.at[0]), pltpu.make_async_copy(g_hbm, g_s, sem.at[1])]
    for i, w_hbm in enumerate((wk_hbm, wq_hbm, wv_hbm, wo_hbm)):
        copies.append(pltpu.make_async_copy(w_hbm.at[0], w_s.at[i], sem.at[2 + i]))
    start_all(copies)
    copies[0].wait()
    copies[1].wait()
    normed = rms_normed(f_s[...], g_s[...]).astype(bf16)
    copies[2].wait()
    kt_s[...] = lax.dot_general(w_s[0].T, normed, NT, preferred_element_type=f32).astype(bf16)
    copies[3].wait()
    q_s[...] = (dot(normed, w_s[1]) * QUERY_FACTOR).astype(bf16)
    copies[4].wait()
    v_s[...] = dot(normed, w_s[2]).astype(bf16)
    copies[5].wait()
    row = lax.broadcasted_iota(jnp.int32, (128, lon), 0) // HEAD
    lane = lax.broadcasted_iota(jnp.int32, (lon, 128), 1) // HEAD

    def attend(shifted):
        acc_s[...] = jnp.zeros_like(acc_s)

        @pl.loop(0, HEADS)
        def _(head):
            half = head // 4
            at = pl.multiple_of(half * 128, 128)
            keys = kt_s[pl.ds(at, 128), :]
            keys = jnp.where(row == head % 4, keys, jnp.zeros_like(keys))
            own = lane == head % 4
            values = v_s[:, pl.ds(at, 128)]
            ones = jnp.where(own, 1.0, 0.0).astype(bf16)
            values = jnp.concatenate([jnp.where(own, values, jnp.zeros_like(values)), ones], axis=1)

            def score(start):
                scores = dot(q_s[start : start + block, pl.ds(at, 128)], keys)
                if shifted:
                    scores = scores - jnp.max(scores, axis=1, keepdims=True)
                return scores

            ahead = score(0)
            for start in range(0, lon, block):
                weights = jnp.exp2(ahead).astype(bf16)
                if start + block < lon:
                    ahead = score(start + block)
                acc_s[half, start : start + block, :] += dot(weights, values)

    attend(False)
    bad = jnp.max(out_of_range(acc_s[:, :, 128:256]))

    @pl.when(bad > 0.0)
    def _():
        attend(True)

    heads = [(acc_s[i, :, 0:128] / acc_s[i, :, 128:256]).astype(bf16) for i in range(2)]
    o_ref[...] = f_s[...].astype(f32) + dot(jnp.concatenate(heads, axis=1), w_s[3])


def lon_row(after, fields, gain, w_query, w_key, w_value, w_out, row_at):
    lon = fields.shape[1]
    return pl.pallas_call(
        functools.partial(lon_kernel, row_at=row_at, block=lon // 2),
        out_shape=jax.ShapeDtypeStruct((lon, D), f32),
        in_specs=[ANY] * 7,
        scratch_shapes=[
            pltpu.VMEM((lon, D), bf16),
            pltpu.VMEM((1, D), f32),
            pltpu.VMEM((4, D, D), bf16),
            pltpu.VMEM((lon, D), bf16),
            pltpu.VMEM((D, lon), bf16),
            pltpu.VMEM((lon, D), bf16),
            pltpu.VMEM((2, lon, D), f32),
            pltpu.SemaphoreType.DMA((6,)),
        ],
        compiler_params=pltpu.CompilerParams(vmem_limit_bytes=VMEM),
        cost_estimate=pl.CostEstimate(flops=25_000_000_000, bytes_accessed=3_000_000, transcendentals=0),
        name="lon",
    )(after, fields, gain, w_query, w_key, w_value, w_out)


def cross_kernel(
    after, x_hbm, wq_hbm, wk_hbm, wv_hbm, wo_hbm, o_hbm,
    in_s, w_s, flat_s, x_s, q_s, k_s, v_s, h_s, bad_s, in_sem, w_sem, out_sem, *, members,
):
    del after
    parts = x_hbm.shape[0]
    groups = parts // members
    seq = 2 * groups
    rows = parts * 2 * PER
    block = members * 2 * PER
    stride = flat_s.shape[1] // groups
    share = parts // STEPS

    loads = [
        pltpu.make_async_copy(x_hbm.at[pl.ds(i * share, share)], in_s.at[pl.ds(i * share, share)], in_sem.at[i])
        for i in range(STEPS)
    ]
    weights_in = []
    for i, w_hbm in enumerate((wq_hbm, wk_hbm, wv_hbm, wo_hbm)):
        weights_in.append(pltpu.make_async_copy(w_hbm.at[pl.ds(1, 2)], w_s.at[i], w_sem.at[i]))
    start_all(loads + weights_in)

    def place(member, j, r):
        inside = r * WIDE + j if j < WIDE else 2 * WIDE + r * NARROW + (j - WIDE)
        return member * 2 * PER + inside

    for i in range(STEPS):
        loads[i].wait()
        for g in range(i * groups // STEPS, (i + 1) * groups // STEPS):
            wide = in_s[g * members : (g + 1) * members].astype(f32).reshape(block, D)
            for c in range(2):
                flat_s[c, g * stride : g * stride + block, :] = wide[:, 128 * c : 128 * c + 128]
    for member in range(members):
        for j in range(PER):
            base = (member * PER + j) * seq
            for c in range(2):
                pieces = [flat_s[c, pl.ds(place(member, j, r), groups, stride=stride), :] for r in range(2)]
                x_s[base : base + seq, 128 * c : 128 * c + 128] = jnp.concatenate(pieces, axis=0).astype(bf16)
    for copy in weights_in:
        copy.wait()

    @pl.loop(0, 3)
    def _(n):
        at = pl.multiple_of(n * (rows // 3), rows // 3)
        x = x_s[pl.ds(at, rows // 3), :]
        for b in range(2):
            q_s[b, pl.ds(at, rows // 3), :] = (dot(x, w_s[0, b]) * QUERY_FACTOR).astype(bf16)
            k_s[b, pl.ds(at, rows // 3), :] = dot(x, w_s[1, b]).astype(bf16)
            v_s[b, pl.ds(at, rows // 3), :] = dot(x, w_s[2, b]).astype(bf16)

    twice = 2 * seq
    own = lax.broadcasted_iota(jnp.int32, (twice, 128), 0) // seq
    own = own == (lax.broadcasted_iota(jnp.int32, (twice, 128), 1) // HEAD) % 2
    ones = jnp.where(own, 1.0, 0.0).astype(bf16)
    left = lax.broadcasted_iota(jnp.int32, (seq, 128), 1) < 64

    def lat_score(spot, shifted):
        at, lanes = spot
        query, key = q_s[0, pl.ds(at, seq), lanes], k_s[0, pl.ds(at, seq), lanes]
        none = jnp.zeros_like(query)
        keys = jnp.concatenate([key, key], axis=0)
        keys = jnp.where(own, keys, jnp.zeros_like(keys))
        queries = jnp.concatenate([jnp.where(left, query, none), jnp.where(left, none, query)], axis=0)
        scores = lax.dot_general(queries, keys, NT, preferred_element_type=f32)
        if shifted:
            first = lax.broadcasted_iota(jnp.int32, scores.shape, 1) < seq
            tops = [jnp.max(jnp.where(first == side, scores, -jnp.inf), axis=1, keepdims=True) for side in (True, False)]
            scores = scores - jnp.where(first, tops[0], tops[1])
        return scores

    def lat_finish(spot, scores):
        at, lanes = spot
        value = v_s[0, pl.ds(at, seq), lanes]
        values = jnp.concatenate([value, value], axis=0)
        values = jnp.where(own, values, jnp.zeros_like(values))
        weights = jnp.exp2(scores).astype(bf16)
        mixed, total = dot(weights, values), dot(weights, ones)
        return jnp.where(left, mixed[:seq], mixed[seq:]), jnp.where(left, total[:seq], total[seq:])

    def lat_attend(shifted, several):
        @pl.loop(0, members * PER // several)
        def _(n):
            spots = [
                (pl.multiple_of((n * several + u) * seq, seq), slice(128 * c, 128 * c + 128))
                for u in range(several)
                for c in range(2)
            ]
            scores = [lat_score(spot, shifted) for spot in spots]
            results = [lat_finish(spot, score) for spot, score in zip(spots, scores)]
            for (at, lanes), (mixed, total) in zip(spots, results):
                h_s[pl.ds(at, seq), lanes] = (mixed / total).astype(bf16)
            if not shifted:
                bad_s[...] = functools.reduce(jnp.maximum, [out_of_range(total) for _, total in results], bad_s[...])

    bad_s[...] = jnp.zeros_like(bad_s)
    lat_attend(False, 8)
    bad = jnp.max(bad_s[...])

    @pl.when(bad > 0.0)
    def _():
        lat_attend(True, 1)

    count = PER * seq
    piece = count // 4
    feature = lax.broadcasted_iota(jnp.int32, (D, 128), 0) // HEAD
    lane = lax.broadcasted_iota(jnp.int32, (D, 128), 1)
    fold = jnp.concatenate(
        [
            jnp.where(lane == n * 32 + m * HEADS + feature, 1.0, 0.0).astype(bf16)
            for m in range(members)
            for n in range(members)
        ],
        axis=0,
    )
    slot = lax.broadcasted_iota(jnp.int32, (128, D), 0)
    feature = lax.broadcasted_iota(jnp.int32, (128, D), 1) // HEAD
    spread = [
        jnp.concatenate(
            [jnp.where(slot == n * 32 + m * HEADS + feature, 1.0, 0.0).astype(bf16) for n in range(members)], axis=1
        )
        for m in range(members)
    ]
    spots = [[i * piece + member * count for member in range(members)] for i in range(4)]

    def over_members(combine, x):
        return functools.reduce(combine, [pltpu.roll(x, 32 * n, 1) for n in (1, 2, 3)], x)

    def mem_weights(ats):
        keys = [k_s[1, at : at + piece, :] for at in ats]
        queries = [q_s[1, at : at + piece, :] for at in ats]
        scores = dot(jnp.concatenate([query * key for query in queries for key in keys], axis=1), fold)
        weights = jnp.exp2(scores - over_members(jnp.maximum, scores))
        return (weights / over_members(jnp.add, weights)).astype(bf16)

    def mem_finish(ats, weights):
        values = [v_s[1, at : at + piece, :].astype(f32) for at in ats]
        for m in range(members):
            wide = dot(weights, spread[m])
            terms = [wide[:, n * D : n * D + D] * values[n] for n in range(members)]
            h_s[ats[m] : ats[m] + piece, D : 2 * D] = functools.reduce(jnp.add, terms).astype(bf16)

    ahead = mem_weights(spots[0])
    for i, ats in enumerate(spots):
        weights = ahead
        if i + 1 < len(spots):
            ahead = mem_weights(spots[i + 1])
        mem_finish(ats, weights)

    for member in range(members):
        base = member * PER * seq
        h = h_s[base : base + PER * seq, :]
        out = dot(h[:, 0:D], w_s[3, 0]) + dot(h[:, D : 2 * D], w_s[3, 1])
        for j in range(PER):
            for c in range(2):
                for r in range(2):
                    at = j * seq + r * groups
                    value = out[at : at + groups, 128 * c : 128 * c + 128]
                    flat_s[c, pl.ds(place(member, j, r), groups, stride=stride), :] = value
    stores = []
    for i in range(STEPS):
        for g in range(i * groups // STEPS, (i + 1) * groups // STEPS):
            both = jnp.concatenate([flat_s[c, g * stride : g * stride + block, :] for c in range(2)], axis=1)
            in_s[g * members : (g + 1) * members] = both.reshape(members, 2 * PER, D).astype(bf16)
        part = pl.ds(i * share, share)
        stores.append(pltpu.make_async_copy(in_s.at[part], o_hbm.at[part], out_sem.at[i]))
        stores[-1].start()
    for copy in stores:
        copy.wait()


def cross(after, received, w_query, w_key, w_value, w_out, members):
    parts = received.shape[0]
    rows = parts * 2 * PER
    groups = parts // members
    return pl.pallas_call(
        functools.partial(cross_kernel, members=members),
        out_shape=jax.ShapeDtypeStruct(received.shape, bf16),
        in_specs=[ANY] * 6,
        out_specs=ANY,
        scratch_shapes=[
            pltpu.VMEM(received.shape, bf16),
            pltpu.VMEM((4, 2, D, D), bf16),
            pltpu.VMEM((2, rows + 8 * groups, 128), f32),
            pltpu.VMEM((rows, D), bf16),
            pltpu.VMEM((2, rows, D), bf16),
            pltpu.VMEM((2, rows, D), bf16),
            pltpu.VMEM((2, rows, D), bf16),
            pltpu.VMEM((rows, 2 * D), bf16),
            pltpu.VMEM((2 * groups, 128), f32),
            pltpu.SemaphoreType.DMA((STEPS,)),
            pltpu.SemaphoreType.DMA((4,)),
            pltpu.SemaphoreType.DMA((STEPS,)),
        ],
        compiler_params=pltpu.CompilerParams(vmem_limit_bytes=VMEM),
        cost_estimate=pl.CostEstimate(flops=12_000_000_000, bytes_accessed=5_000_000, transcendentals=0),
        name="cross",
    )(after, received, w_query, w_key, w_value, w_out)


def on_device(fields, norm_gain, w_query, w_key, w_value, w_out, *, lat, members):
    state = fields.reshape(fields.shape[1:])
    gain = norm_gain.reshape(1, D)
    axes = ("lat", "mem")
    weights = (w_query, w_key, w_value, w_out)
    packed = pack(state, gain, lat * members)
    received = lax.all_to_all(packed, axes, split_axis=0, concat_axis=0, tiled=True)
    part0 = lon_row(packed, state, gain, *weights, 0)
    sent = cross(part0, received, *weights, members)
    returned = lax.all_to_all(sent, axes, split_axis=0, concat_axis=0, tiled=True)
    part1 = lon_row(sent, state, gain, *weights, 1)
    return unpack(part0, part1, returned).reshape(fields.shape)


def solution(mesh):
    return jax.shard_map(
        functools.partial(on_device, lat=mesh.shape["lat"], members=mesh.shape["mem"]),
        mesh=mesh,
        in_specs=(P("mem", "lat", None, None), P(), P(), P(), P(), P()),
        out_specs=P("mem", "lat", None, None),
        check_vma=False,
    )
```

```python
import functools
import math

import jax
import jax.numpy as jnp
from jax import lax
from jax.experimental import pallas as pl
from jax.experimental.pallas import tpu as pltpu
from jax.sharding import PartitionSpec as P

HEADS = 8
HEAD = 32
D = 256
EPSILON = 1e-06
QUERY_FACTOR = math.log2(math.e) / math.sqrt(HEAD)
LOW, HIGH = 2.0**-100, 2.0**120
NT = (((1,), (1,)), ((), ()))
MIB = 2**20
WIDE, NARROW = 8, 4
PER = WIDE + NARROW
STEPS = 4
VMEM = 60 * MIB

f32, bf16 = jnp.float32, jnp.bfloat16


def rms_normed(fields, gain):
    wide = fields.astype(f32)
    meansq = jnp.mean(wide * wide, axis=-1, keepdims=True)
    return wide * lax.rsqrt(meansq + EPSILON) * gain


def dot(a, b):
    return jnp.dot(a, b, preferred_element_type=f32)


ANY = pl.BlockSpec(memory_space=pl.ANY)


def start_all(copies):
    for copy in copies:
        copy.start()
    return copies


def spans(step, parts, lon):
    count = parts // STEPS
    cut = parts * WIDE
    narrow = cut + step * count * NARROW
    return (
        (step * count, count),
        (step * count * WIDE, count * WIDE),
        (narrow, max(0, min(count * NARROW, lon - narrow))),
    )


def pack_kernel(f_hbm, g_hbm, o_ref, f_s, g_s, sem, g_sem, *, parts):
    lon = f_hbm.shape[1]
    all_spans = [spans(step, parts, lon) for step in range(STEPS)]
    gain_copy = pltpu.make_async_copy(g_hbm, g_s, g_sem)
    gain_copy.start()
    copies = [
        start_all(
            [
                pltpu.make_async_copy(f_hbm.at[:, pl.ds(at, n)], f_s.at[:, pl.ds(at, n)], sem.at[step, i])
                for i, (at, n) in enumerate(all_spans[step][1:])
                if n
            ]
        )
        for step in range(STEPS)
    ]
    gain_copy.wait()
    gain = g_s[...]
    for step, ((dev, count), (at, n), (at2, n2)) in enumerate(all_spans):
        for copy in copies[step]:
            copy.wait()
        first = [rms_normed(f_s[r, at : at + n, :], gain).reshape(count, WIDE, D) for r in range(2)]
        o_ref[dev : dev + count, 0:16, :] = jnp.concatenate(first, axis=1).astype(bf16)
        have = n2 // NARROW
        if have:
            a, b = [rms_normed(f_s[r, at2 : at2 + n2, :], gain).reshape(have // 2, 8, D) for r in range(2)]
            upper = lax.broadcasted_iota(jnp.int32, a.shape, 1) < 4
            even = jnp.where(upper, a, pltpu.roll(b, 4, 1))
            odd = jnp.where(upper, pltpu.roll(a, 4, 1), b)
            both = jnp.stack([even, odd], axis=1).reshape(have, 8, D)
            o_ref[dev : dev + have, 16:24, :] = both.astype(bf16)
        if have < count:
            o_ref[dev + have : dev + count, 16:24, :] = jnp.zeros((count - have, 8, D), bf16)


def pack(fields, gain, parts):
    return pl.pallas_call(
        functools.partial(pack_kernel, parts=parts),
        out_shape=jax.ShapeDtypeStruct((parts, 2 * PER, D), bf16),
        in_specs=[ANY, ANY],
        scratch_shapes=[
            pltpu.VMEM(fields.shape, bf16),
            pltpu.VMEM((1, D), f32),
            pltpu.SemaphoreType.DMA((STEPS, 2)),
            pltpu.SemaphoreType.DMA,
        ],
        compiler_params=pltpu.CompilerParams(vmem_limit_bytes=60 * MIB),
        cost_estimate=pl.CostEstimate(flops=4_000_000, bytes_accessed=3_000_000, transcendentals=0),
        name="pack",
    )(fields, gain)


def unpack_kernel(p_ref, x_ref, o_ref):
    parts, lon = x_ref.shape[0], o_ref.shape[1]
    for step in range(STEPS):
        (dev, count), (at, n), (at2, n2) = spans(step, parts, lon)
        first = x_ref[dev : dev + count, 0:16, :].astype(f32)
        for r in range(2):
            add = first[:, 8 * r : 8 * r + 8, :].reshape(n, D)
            o_ref[r, at : at + n, :] = (p_ref[r, at : at + n, :].astype(f32) + add).astype(bf16)
        have = n2 // NARROW
        if have:
            both = x_ref[dev : dev + have, 16:24, :].astype(f32).reshape(have // 2, 2, 8, D)
            even, odd = both[:, 0], both[:, 1]
            upper = lax.broadcasted_iota(jnp.int32, even.shape, 1) < 4
            rows = (jnp.where(upper, even, pltpu.roll(odd, 4, 1)), jnp.where(upper, pltpu.roll(even, 4, 1), odd))
            for r in range(2):
                add = rows[r].reshape(n2, D)
                o_ref[r, at2 : at2 + n2, :] = (p_ref[r, at2 : at2 + n2, :].astype(f32) + add).astype(bf16)


def unpack(partial, returned):
    return pl.pallas_call(
        unpack_kernel,
        out_shape=jax.ShapeDtypeStruct(partial.shape, bf16),
        compiler_params=pltpu.CompilerParams(vmem_limit_bytes=40 * MIB),
        cost_estimate=pl.CostEstimate(flops=4_000_000, bytes_accessed=6_000_000, transcendentals=0),
        name="unpack",
    )(partial, returned)


def out_of_range(total):
    return jnp.where((total > LOW) & (total < HIGH), 0.0, 1.0)


def lon_kernel(after, f_hbm, g_hbm, wq_hbm, wk_hbm, wv_hbm, wo_hbm, *refs, row_at):
    o_hbm, f_s, g_s, w_s, x_s, q_s, kt_s, v_s, kb_s, vb_s, acc_s, o_s, f_sem, w_sem, o_sem = refs[-15:]
    del after
    lon = f_s.shape[0]
    main = lon // 256 * 256
    rest = lon - main
    thirds = [slice(lon // 3 * i, lon // 3 * (i + 1)) for i in range(3)]
    g_copy = pltpu.make_async_copy(g_hbm, g_s, f_sem.at[3])
    f_copies = [pltpu.make_async_copy(f_hbm.at[row_at, at], f_s.at[at], f_sem.at[i]) for i, at in enumerate(thirds)]
    w_copies = [
        pltpu.make_async_copy(w_hbm.at[0], w_s.at[i], w_sem.at[i])
        for i, w_hbm in enumerate((wk_hbm, wq_hbm, wv_hbm, wo_hbm))
    ]
    start_all([g_copy] + f_copies + w_copies)
    g_copy.wait()
    for i, at in enumerate(thirds):
        f_copies[i].wait()
        x_s[at, :] = rms_normed(f_s[at, :], g_s[...]).astype(bf16)
    w_copies[0].wait()
    kt_s[...] = lax.dot_general(w_s[0].T, x_s[...], NT, preferred_element_type=f32).astype(bf16)
    w_copies[1].wait()
    q_s[...] = (dot(x_s[...], w_s[1]) * QUERY_FACTOR).astype(bf16)
    w_copies[2].wait()
    v_s[...] = dot(x_s[...], w_s[2]).astype(bf16)
    w_copies[3].wait()
    key_rest = dot(x_s[main:lon, :], w_s[0]).astype(bf16)
    value_rest = v_s[main:lon, :]
    lane_rest = lax.broadcasted_iota(jnp.int32, (rest, D), 1) // HEAD
    for head in range(HEADS):
        own = lane_rest == head
        half, slot = head // 4, head % 4
        kb_s[head * rest : (head + 1) * rest, :] = jnp.where(own, key_rest, jnp.zeros_like(key_rest))
        mine = slice(128 * half, 128 * half + 128)
        values = jnp.where(own, value_rest, jnp.zeros_like(value_rest))[:, mine]
        ones = jnp.where(own, 1.0, 0.0).astype(bf16)[:, mine]
        vb_s[half, slot * rest : (slot + 1) * rest, :] = jnp.concatenate([values, ones], axis=1)
    row = lax.broadcasted_iota(jnp.int32, (128, lon), 0) // HEAD
    lane = lax.broadcasted_iota(jnp.int32, (lon, 128), 1) // HEAD
    block = lon // 2

    def attend(shifted):
        keyed = lon if shifted else main
        acc_s[...] = jnp.zeros_like(acc_s)

        @pl.loop(0, HEADS)
        def _(head):
            half = head // 4
            at = pl.multiple_of(half * 128, 128)
            keys = kt_s[pl.ds(at, 128), 0:keyed]
            keys = jnp.where(row[:, 0:keyed] == head % 4, keys, jnp.zeros_like(keys))
            own = lane[0:keyed] == head % 4
            values = v_s[0:keyed, pl.ds(at, 128)]
            ones = jnp.where(own, 1.0, 0.0).astype(bf16)
            values = jnp.concatenate([jnp.where(own, values, jnp.zeros_like(values)), ones], axis=1)

            def score(start):
                scores = dot(q_s[start : start + block, pl.ds(at, 128)], keys)
                if shifted:
                    scores = scores - jnp.max(scores, axis=1, keepdims=True)
                return scores

            ahead = score(0)
            for start in range(0, lon, block):
                weights = jnp.exp2(ahead).astype(bf16)
                if start + block < lon:
                    ahead = score(start + block)
                acc_s[half, start : start + block, :] += dot(weights, values)

    attend(False)

    def score_rest(at):
        return lax.dot_general(q_s[at, :], kb_s[...], NT, preferred_element_type=f32)

    ahead = score_rest(thirds[0])
    for i, at in enumerate(thirds):
        weights = jnp.exp2(ahead).astype(bf16)
        if i + 1 < len(thirds):
            ahead = score_rest(thirds[i + 1])
        for half in range(2):
            acc_s[half, at, :] += dot(weights[:, 4 * rest * half : 4 * rest * (half + 1)], vb_s[half])
    bad = jnp.max(out_of_range(acc_s[:, :, 128:256]))

    @pl.when(bad > 0.0)
    def _():
        attend(True)

    stores = []
    for i, at in enumerate(thirds):
        heads = [(acc_s[c, at, 0:128] / acc_s[c, at, 128:256]).astype(bf16) for c in range(2)]
        o_s[at, :] = (f_s[at, :].astype(f32) + dot(jnp.concatenate(heads, axis=1), w_s[3])).astype(bf16)
        stores.append(pltpu.make_async_copy(o_s.at[at], o_hbm.at[row_at, at], o_sem.at[i]))
        stores[-1].start()
    for copy in stores:
        copy.wait()


def lon_row(after, fields, gain, w_query, w_key, w_value, w_out, row_at, other=()):
    lon = fields.shape[1]
    rest = lon % 256
    return pl.pallas_call(
        functools.partial(lon_kernel, row_at=row_at),
        out_shape=jax.ShapeDtypeStruct(fields.shape, bf16),
        in_specs=[ANY] * (7 + len(other)),
        out_specs=ANY,
        input_output_aliases={7: 0} if other else {},
        scratch_shapes=[
            pltpu.VMEM((lon, D), bf16),
            pltpu.VMEM((1, D), f32),
            pltpu.VMEM((4, D, D), bf16),
            pltpu.VMEM((lon, D), bf16),
            pltpu.VMEM((lon, D), bf16),
            pltpu.VMEM((D, lon), bf16),
            pltpu.VMEM((lon, D), bf16),
            pltpu.VMEM((HEADS * rest, D), bf16),
            pltpu.VMEM((2, HEADS // 2 * rest, D), bf16),
            pltpu.VMEM((2, lon, D), f32),
            pltpu.VMEM((lon, D), bf16),
            pltpu.SemaphoreType.DMA((4,)),
            pltpu.SemaphoreType.DMA((4,)),
            pltpu.SemaphoreType.DMA((3,)),
        ],
        compiler_params=pltpu.CompilerParams(vmem_limit_bytes=60 * MIB),
        cost_estimate=pl.CostEstimate(flops=25_000_000_000, bytes_accessed=3_000_000, transcendentals=0),
        name="lon",
    )(after, fields, gain, w_query, w_key, w_value, w_out, *other)


def cross_kernel(
    x_ref, wq_hbm, wk_hbm, wv_hbm, wo_hbm, o_hbm,
    in_s, w_s, flat_s, x_s, q_s, k_s, v_s, h_s, bad_s, w_sem, out_sem, *, members,
):
    parts = x_ref.shape[0]
    groups = parts // members
    seq = 2 * groups
    rows = parts * 2 * PER
    block = members * 2 * PER
    stride = flat_s.shape[1] // groups
    share = parts // STEPS

    weights_in = []
    for i, w_hbm in enumerate((wq_hbm, wk_hbm, wv_hbm, wo_hbm)):
        weights_in.append(pltpu.make_async_copy(w_hbm.at[pl.ds(1, 2)], w_s.at[i], w_sem.at[i]))
    start_all(weights_in)

    def place(member, j, r):
        inside = r * WIDE + j if j < WIDE else 2 * WIDE + r * NARROW + (j - WIDE)
        return member * 2 * PER + inside

    for i in range(STEPS):
        for g in range(i * groups // STEPS, (i + 1) * groups // STEPS):
            wide = x_ref[g * members : (g + 1) * members].astype(f32).reshape(block, D)
            for c in range(2):
                flat_s[c, g * stride : g * stride + block, :] = wide[:, 128 * c : 128 * c + 128]
    for member in range(members):
        for j in range(PER):
            base = (member * PER + j) * seq
            for c in range(2):
                pieces = [flat_s[c, pl.ds(place(member, j, r), groups, stride=stride), :] for r in range(2)]
                x_s[base : base + seq, 128 * c : 128 * c + 128] = jnp.concatenate(pieces, axis=0).astype(bf16)
    for copy in weights_in:
        copy.wait()

    @pl.loop(0, 3)
    def _(n):
        at = pl.multiple_of(n * (rows // 3), rows // 3)
        x = x_s[pl.ds(at, rows // 3), :]
        for b in range(2):
            q_s[b, pl.ds(at, rows // 3), :] = (dot(x, w_s[0, b]) * QUERY_FACTOR).astype(bf16)
            k_s[b, pl.ds(at, rows // 3), :] = dot(x, w_s[1, b]).astype(bf16)
            v_s[b, pl.ds(at, rows // 3), :] = dot(x, w_s[2, b]).astype(bf16)

    twice = 2 * seq
    own = lax.broadcasted_iota(jnp.int32, (twice, 128), 0) // seq
    own = own == (lax.broadcasted_iota(jnp.int32, (twice, 128), 1) // HEAD) % 2
    ones = jnp.where(own, 1.0, 0.0).astype(bf16)
    left = lax.broadcasted_iota(jnp.int32, (seq, 128), 1) < 64

    def lat_score(spot, shifted):
        at, lanes = spot
        query, key = q_s[0, pl.ds(at, seq), lanes], k_s[0, pl.ds(at, seq), lanes]
        none = jnp.zeros_like(query)
        keys = jnp.concatenate([key, key], axis=0)
        keys = jnp.where(own, keys, jnp.zeros_like(keys))
        queries = jnp.concatenate([jnp.where(left, query, none), jnp.where(left, none, query)], axis=0)
        scores = lax.dot_general(queries, keys, NT, preferred_element_type=f32)
        if shifted:
            first = lax.broadcasted_iota(jnp.int32, scores.shape, 1) < seq
            tops = [jnp.max(jnp.where(first == side, scores, -jnp.inf), axis=1, keepdims=True) for side in (True, False)]
            scores = scores - jnp.where(first, tops[0], tops[1])
        return scores

    def lat_finish(spot, scores):
        at, lanes = spot
        value = v_s[0, pl.ds(at, seq), lanes]
        values = jnp.concatenate([value, value], axis=0)
        values = jnp.where(own, values, jnp.zeros_like(values))
        weights = jnp.exp2(scores).astype(bf16)
        mixed, total = dot(weights, values), dot(weights, ones)
        return jnp.where(left, mixed[:seq], mixed[seq:]), jnp.where(left, total[:seq], total[seq:])

    def lat_attend(shifted, several):
        @pl.loop(0, members * PER // several)
        def _(n):
            spots = [
                (pl.multiple_of((n * several + u) * seq, seq), slice(128 * c, 128 * c + 128))
                for u in range(several)
                for c in range(2)
            ]
            scores = [lat_score(spot, shifted) for spot in spots]
            results = [lat_finish(spot, score) for spot, score in zip(spots, scores)]
            for (at, lanes), (mixed, total) in zip(spots, results):
                h_s[pl.ds(at, seq), lanes] = (mixed / total).astype(bf16)
            if not shifted:
                bad_s[...] = functools.reduce(jnp.maximum, [out_of_range(total) for _, total in results], bad_s[...])

    bad_s[...] = jnp.zeros_like(bad_s)
    lat_attend(False, 8)
    bad = jnp.max(bad_s[...])

    @pl.when(bad > 0.0)
    def _():
        lat_attend(True, 1)

    count = PER * seq
    piece = count // 4
    feature = lax.broadcasted_iota(jnp.int32, (D, 128), 0) // HEAD
    lane = lax.broadcasted_iota(jnp.int32, (D, 128), 1)
    fold = jnp.concatenate(
        [
            jnp.where(lane == n * 32 + m * HEADS + feature, 1.0, 0.0).astype(bf16)
            for m in range(members)
            for n in range(members)
        ],
        axis=0,
    )
    slot = lax.broadcasted_iota(jnp.int32, (128, D), 0)
    feature = lax.broadcasted_iota(jnp.int32, (128, D), 1) // HEAD
    spread = [
        jnp.concatenate(
            [jnp.where(slot == n * 32 + m * HEADS + feature, 1.0, 0.0).astype(bf16) for n in range(members)], axis=1
        )
        for m in range(members)
    ]
    spots = [[i * piece + member * count for member in range(members)] for i in range(4)]

    def over_members(combine, x):
        return functools.reduce(combine, [pltpu.roll(x, 32 * n, 1) for n in (1, 2, 3)], x)

    def mem_weights(ats):
        keys = [k_s[1, at : at + piece, :] for at in ats]
        queries = [q_s[1, at : at + piece, :] for at in ats]
        scores = dot(jnp.concatenate([query * key for query in queries for key in keys], axis=1), fold)
        weights = jnp.exp2(scores - over_members(jnp.maximum, scores))
        return (weights / over_members(jnp.add, weights)).astype(bf16)

    def mem_finish(ats, weights):
        values = [v_s[1, at : at + piece, :].astype(f32) for at in ats]
        for m in range(members):
            wide = dot(weights, spread[m])
            terms = [wide[:, n * D : n * D + D] * values[n] for n in range(members)]
            h_s[ats[m] : ats[m] + piece, D : 2 * D] = functools.reduce(jnp.add, terms).astype(bf16)

    ahead = mem_weights(spots[0])
    for i, ats in enumerate(spots):
        weights = ahead
        if i + 1 < len(spots):
            ahead = mem_weights(spots[i + 1])
        mem_finish(ats, weights)

    for member in range(members):
        base = member * PER * seq
        h = h_s[base : base + PER * seq, :]
        out = dot(h[:, 0:D], w_s[3, 0]) + dot(h[:, D : 2 * D], w_s[3, 1])
        for j in range(PER):
            for c in range(2):
                for r in range(2):
                    at = j * seq + r * groups
                    value = out[at : at + groups, 128 * c : 128 * c + 128]
                    flat_s[c, pl.ds(place(member, j, r), groups, stride=stride), :] = value
    stores = []
    for i in range(STEPS):
        for g in range(i * groups // STEPS, (i + 1) * groups // STEPS):
            both = jnp.concatenate([flat_s[c, g * stride : g * stride + block, :] for c in range(2)], axis=1)
            in_s[g * members : (g + 1) * members] = both.reshape(members, 2 * PER, D).astype(bf16)
        part = pl.ds(i * share, share)
        stores.append(pltpu.make_async_copy(in_s.at[part], o_hbm.at[part], out_sem.at[i]))
        stores[-1].start()
    for copy in stores:
        copy.wait()


def cross(received, w_query, w_key, w_value, w_out, members):
    parts = received.shape[0]
    rows = parts * 2 * PER
    groups = parts // members
    return pl.pallas_call(
        functools.partial(cross_kernel, members=members),
        out_shape=jax.ShapeDtypeStruct(received.shape, bf16),
        in_specs=[pl.BlockSpec(memory_space=pltpu.VMEM)] + [ANY] * 4,
        out_specs=ANY,
        scratch_shapes=[
            pltpu.VMEM(received.shape, bf16),
            pltpu.VMEM((4, 2, D, D), bf16),
            pltpu.VMEM((2, rows + 8 * groups, 128), f32),
            pltpu.VMEM((rows, D), bf16),
            pltpu.VMEM((2, rows, D), bf16),
            pltpu.VMEM((2, rows, D), bf16),
            pltpu.VMEM((2, rows, D), bf16),
            pltpu.VMEM((rows, 2 * D), bf16),
            pltpu.VMEM((2 * groups, 128), f32),
            pltpu.SemaphoreType.DMA((4,)),
            pltpu.SemaphoreType.DMA((STEPS,)),
        ],
        compiler_params=pltpu.CompilerParams(vmem_limit_bytes=40 * MIB),
        cost_estimate=pl.CostEstimate(flops=12_000_000_000, bytes_accessed=5_000_000, transcendentals=0),
        name="cross",
    )(received, w_query, w_key, w_value, w_out)


def on_device(fields, norm_gain, w_query, w_key, w_value, w_out, *, lat, members):
    state = fields.reshape(fields.shape[1:])
    gain = norm_gain.reshape(1, D)
    axes = ("lat", "mem")
    weights = (w_query, w_key, w_value, w_out)
    packed = pack(state, gain, lat * members)
    received = lax.all_to_all(packed, axes, split_axis=0, concat_axis=0, tiled=True)
    partial = lon_row(packed, state, gain, *weights, 0)
    sent = cross(received, *weights, members)
    returned = lax.all_to_all(sent, axes, split_axis=0, concat_axis=0, tiled=True)
    partial = lon_row(sent, state, gain, *weights, 1, (partial,))
    return unpack(partial, returned).reshape(fields.shape)


def solution(mesh):
    return jax.shard_map(
        functools.partial(on_device, lat=mesh.shape["lat"], members=mesh.shape["mem"]),
        mesh=mesh,
        in_specs=(P("mem", "lat", None, None), P(), P(), P(), P(), P()),
        out_specs=P("mem", "lat", None, None),
        check_vma=False,
    )
```

```python
import functools
import math

import jax
import jax.numpy as jnp
from jax import lax
from jax.experimental import pallas as pl
from jax.experimental.pallas import tpu as pltpu
from jax.sharding import PartitionSpec as P

HEADS = 8
HEAD = 32
D = 256
EPSILON = 1e-06
QUERY_FACTOR = math.log2(math.e) / math.sqrt(HEAD)
LOW, HIGH = 2.0**-100, 2.0**120
NT = (((1,), (1,)), ((), ()))
MIB = 2**20
WIDE, NARROW = 8, 4
PER = WIDE + NARROW
STEPS = 8

f32, bf16 = jnp.float32, jnp.bfloat16


def rms_normed(fields, gain):
    wide = fields.astype(f32)
    meansq = jnp.mean(wide * wide, axis=-1, keepdims=True)
    return wide * lax.rsqrt(meansq + EPSILON) * gain


def dot(a, b):
    return jnp.dot(a, b, preferred_element_type=f32)


ANY = pl.BlockSpec(memory_space=pl.ANY)


def start_all(copies):
    for copy in copies:
        copy.start()
    return copies


def spans(step, parts, lon):
    count = parts // STEPS
    cut = parts * WIDE
    narrow = cut + step * count * NARROW
    return (
        (step * count, count),
        (step * count * WIDE, count * WIDE),
        (narrow, max(0, min(count * NARROW, lon - narrow))),
    )


def pack_kernel(f_hbm, g_hbm, o_hbm, f_s, g_s, o_s, sem, g_sem, o_sem, *, parts):
    lon = f_hbm.shape[1]
    all_spans = [spans(step, parts, lon) for step in range(STEPS)]
    gain_copy = pltpu.make_async_copy(g_hbm, g_s, g_sem)
    gain_copy.start()
    copies = [
        start_all(
            [
                pltpu.make_async_copy(f_hbm.at[:, pl.ds(at, n)], f_s.at[:, pl.ds(at, n)], sem.at[step, i])
                for i, (at, n) in enumerate(all_spans[step][1:])
                if n
            ]
        )
        for step in range(STEPS)
    ]
    gain_copy.wait()
    gain = g_s[...]
    stores = []
    for step, ((dev, count), (at, n), (at2, n2)) in enumerate(all_spans):
        for copy in copies[step]:
            copy.wait()
        first = [rms_normed(f_s[r, at : at + n, :], gain).reshape(count, WIDE, D) for r in range(2)]
        o_s[dev : dev + count, 0:16, :] = jnp.concatenate(first, axis=1).astype(bf16)
        have = n2 // NARROW
        if have:
            a, b = [rms_normed(f_s[r, at2 : at2 + n2, :], gain).reshape(have // 2, 8, D) for r in range(2)]
            upper = lax.broadcasted_iota(jnp.int32, a.shape, 1) < 4
            even = jnp.where(upper, a, pltpu.roll(b, 4, 1))
            odd = jnp.where(upper, pltpu.roll(a, 4, 1), b)
            both = jnp.stack([even, odd], axis=1).reshape(have, 8, D)
            o_s[dev : dev + have, 16:24, :] = both.astype(bf16)
        if have < count:
            o_s[dev + have : dev + count, 16:24, :] = jnp.zeros((count - have, 8, D), bf16)
        part = pl.ds(dev, count)
        stores.append(pltpu.make_async_copy(o_s.at[part], o_hbm.at[part], o_sem.at[step]))
        stores[-1].start()
    for copy in stores:
        copy.wait()


def pack(fields, gain, parts):
    return pl.pallas_call(
        functools.partial(pack_kernel, parts=parts),
        out_shape=jax.ShapeDtypeStruct((parts, 2 * PER, D), bf16),
        in_specs=[ANY, ANY],
        out_specs=ANY,
        scratch_shapes=[
            pltpu.VMEM(fields.shape, bf16),
            pltpu.VMEM((1, D), f32),
            pltpu.VMEM((parts, 2 * PER, D), bf16),
            pltpu.SemaphoreType.DMA((STEPS, 2)),
            pltpu.SemaphoreType.DMA,
            pltpu.SemaphoreType.DMA((STEPS,)),
        ],
        compiler_params=pltpu.CompilerParams(vmem_limit_bytes=60 * MIB),
        cost_estimate=pl.CostEstimate(flops=4_000_000, bytes_accessed=3_000_000, transcendentals=0),
        name="pack",
    )(fields, gain)


def unpack_kernel(p_hbm, x_ref, o_hbm, p_s, in_sem, out_sem):
    parts, lon = x_ref.shape[0], p_hbm.shape[1]
    all_spans = [spans(step, parts, lon) for step in range(STEPS)]
    loads = []
    for step, (_, *lons) in enumerate(all_spans):
        mine = [
            pltpu.make_async_copy(p_hbm.at[:, pl.ds(at, n)], p_s.at[:, pl.ds(at, n)], in_sem.at[step, i])
            for i, (at, n) in enumerate(lons)
            if n
        ]
        loads.append(start_all(mine))
    stores = []
    for step, ((dev, count), *lons) in enumerate(all_spans):
        (at, n), (at2, n2) = lons
        for copy in loads[step]:
            copy.wait()
        first = x_ref[dev : dev + count, 0:16, :].astype(f32)
        for r in range(2):
            add = first[:, 8 * r : 8 * r + 8, :].reshape(n, D)
            p_s[r, at : at + n, :] = (p_s[r, at : at + n, :].astype(f32) + add).astype(bf16)
        have = n2 // NARROW
        if have:
            both = x_ref[dev : dev + have, 16:24, :].astype(f32).reshape(have // 2, 2, 8, D)
            even, odd = both[:, 0], both[:, 1]
            upper = lax.broadcasted_iota(jnp.int32, even.shape, 1) < 4
            rows = (jnp.where(upper, even, pltpu.roll(odd, 4, 1)), jnp.where(upper, pltpu.roll(even, 4, 1), odd))
            for r in range(2):
                add = rows[r].reshape(n2, D)
                p_s[r, at2 : at2 + n2, :] = (p_s[r, at2 : at2 + n2, :].astype(f32) + add).astype(bf16)
        for i, (to, m) in enumerate(lons):
            if m:
                part = pl.ds(to, m)
                copy = pltpu.make_async_copy(p_s.at[:, part], o_hbm.at[:, part], out_sem.at[step, i])
                copy.start()
                stores.append(copy)
    for copy in stores:
        copy.wait()


def unpack(partial, returned):
    return pl.pallas_call(
        unpack_kernel,
        out_shape=jax.ShapeDtypeStruct(partial.shape, bf16),
        in_specs=[ANY, pl.BlockSpec(memory_space=pltpu.VMEM)],
        out_specs=ANY,
        input_output_aliases={0: 0},
        scratch_shapes=[
            pltpu.VMEM(partial.shape, bf16),
            pltpu.SemaphoreType.DMA((STEPS, 2)),
            pltpu.SemaphoreType.DMA((STEPS, 2)),
        ],
        compiler_params=pltpu.CompilerParams(vmem_limit_bytes=40 * MIB),
        cost_estimate=pl.CostEstimate(flops=4_000_000, bytes_accessed=6_000_000, transcendentals=0),
        name="unpack",
    )(partial, returned)


def out_of_range(total):
    return jnp.where((total > LOW) & (total < HIGH), 0.0, 1.0)


def lon_kernel(after, f_hbm, g_hbm, wq_hbm, wk_hbm, wv_hbm, wo_hbm, *refs, row_at):
    o_hbm, f_s, g_s, w_s, x_s, q_s, kt_s, v_s, kb_s, vb_s, acc_s, o_s, f_sem, w_sem, o_sem = refs[-15:]
    del after
    lon = f_s.shape[0]
    main = lon // 256 * 256
    rest = lon - main
    thirds = [slice(lon // 3 * i, lon // 3 * (i + 1)) for i in range(3)]
    g_copy = pltpu.make_async_copy(g_hbm, g_s, f_sem.at[3])
    f_copies = [pltpu.make_async_copy(f_hbm.at[row_at, at], f_s.at[at], f_sem.at[i]) for i, at in enumerate(thirds)]
    w_copies = [
        pltpu.make_async_copy(w_hbm.at[0], w_s.at[i], w_sem.at[i])
        for i, w_hbm in enumerate((wk_hbm, wq_hbm, wv_hbm, wo_hbm))
    ]
    start_all([g_copy] + f_copies + w_copies)
    g_copy.wait()
    for i, at in enumerate(thirds):
        f_copies[i].wait()
        x_s[at, :] = rms_normed(f_s[at, :], g_s[...]).astype(bf16)
    w_copies[0].wait()
    kt_s[...] = lax.dot_general(w_s[0].T, x_s[...], NT, preferred_element_type=f32).astype(bf16)
    w_copies[1].wait()
    q_s[...] = (dot(x_s[...], w_s[1]) * QUERY_FACTOR).astype(bf16)
    w_copies[2].wait()
    v_s[...] = dot(x_s[...], w_s[2]).astype(bf16)
    w_copies[3].wait()
    key_rest = dot(x_s[main:lon, :], w_s[0]).astype(bf16)
    value_rest = v_s[main:lon, :]
    lane_rest = lax.broadcasted_iota(jnp.int32, (rest, D), 1) // HEAD
    for head in range(HEADS):
        own = lane_rest == head
        half, slot = head // 4, head % 4
        kb_s[head * rest : (head + 1) * rest, :] = jnp.where(own, key_rest, jnp.zeros_like(key_rest))
        mine = slice(128 * half, 128 * half + 128)
        values = jnp.where(own, value_rest, jnp.zeros_like(value_rest))[:, mine]
        ones = jnp.where(own, 1.0, 0.0).astype(bf16)[:, mine]
        vb_s[half, slot * rest : (slot + 1) * rest, :] = jnp.concatenate([values, ones], axis=1)
    row = lax.broadcasted_iota(jnp.int32, (128, lon), 0) // HEAD
    lane = lax.broadcasted_iota(jnp.int32, (lon, 128), 1) // HEAD
    block = lon // 2

    def attend(shifted):
        keyed = lon if shifted else main
        acc_s[...] = jnp.zeros_like(acc_s)

        @pl.loop(0, HEADS)
        def _(head):
            half = head // 4
            at = pl.multiple_of(half * 128, 128)
            keys = kt_s[pl.ds(at, 128), 0:keyed]
            keys = jnp.where(row[:, 0:keyed] == head % 4, keys, jnp.zeros_like(keys))
            own = lane[0:keyed] == head % 4
            values = v_s[0:keyed, pl.ds(at, 128)]
            ones = jnp.where(own, 1.0, 0.0).astype(bf16)
            values = jnp.concatenate([jnp.where(own, values, jnp.zeros_like(values)), ones], axis=1)

            def score(start):
                scores = dot(q_s[start : start + block, pl.ds(at, 128)], keys)
                if shifted:
                    scores = scores - jnp.max(scores, axis=1, keepdims=True)
                return scores

            ahead = score(0)
            for start in range(0, lon, block):
                weights = jnp.exp2(ahead).astype(bf16)
                if start + block < lon:
                    ahead = score(start + block)
                acc_s[half, start : start + block, :] += dot(weights, values)

    attend(False)

    def score_rest(at):
        return lax.dot_general(q_s[at, :], kb_s[...], NT, preferred_element_type=f32)

    ahead = score_rest(thirds[0])
    for i, at in enumerate(thirds):
        weights = jnp.exp2(ahead).astype(bf16)
        if i + 1 < len(thirds):
            ahead = score_rest(thirds[i + 1])
        for half in range(2):
            acc_s[half, at, :] += dot(weights[:, 4 * rest * half : 4 * rest * (half + 1)], vb_s[half])
    bad = jnp.max(out_of_range(acc_s[:, :, 128:256]))

    @pl.when(bad > 0.0)
    def _():
        attend(True)

    stores = []
    for i, at in enumerate(thirds):
        heads = [(acc_s[c, at, 0:128] / acc_s[c, at, 128:256]).astype(bf16) for c in range(2)]
        o_s[at, :] = (f_s[at, :].astype(f32) + dot(jnp.concatenate(heads, axis=1), w_s[3])).astype(bf16)
        stores.append(pltpu.make_async_copy(o_s.at[at], o_hbm.at[row_at, at], o_sem.at[i]))
        stores[-1].start()
    for copy in stores:
        copy.wait()


def lon_row(after, fields, gain, w_query, w_key, w_value, w_out, row_at, other=()):
    lon = fields.shape[1]
    rest = lon % 256
    return pl.pallas_call(
        functools.partial(lon_kernel, row_at=row_at),
        out_shape=jax.ShapeDtypeStruct(fields.shape, bf16),
        in_specs=[ANY] * (7 + len(other)),
        out_specs=ANY,
        input_output_aliases={7: 0} if other else {},
        scratch_shapes=[
            pltpu.VMEM((lon, D), bf16),
            pltpu.VMEM((1, D), f32),
            pltpu.VMEM((4, D, D), bf16),
            pltpu.VMEM((lon, D), bf16),
            pltpu.VMEM((lon, D), bf16),
            pltpu.VMEM((D, lon), bf16),
            pltpu.VMEM((lon, D), bf16),
            pltpu.VMEM((HEADS * rest, D), bf16),
            pltpu.VMEM((2, HEADS // 2 * rest, D), bf16),
            pltpu.VMEM((2, lon, D), f32),
            pltpu.VMEM((lon, D), bf16),
            pltpu.SemaphoreType.DMA((4,)),
            pltpu.SemaphoreType.DMA((4,)),
            pltpu.SemaphoreType.DMA((3,)),
        ],
        compiler_params=pltpu.CompilerParams(vmem_limit_bytes=60 * MIB),
        cost_estimate=pl.CostEstimate(flops=25_000_000_000, bytes_accessed=3_000_000, transcendentals=0),
        name="lon",
    )(after, fields, gain, w_query, w_key, w_value, w_out, *other)


def cross_kernel(
    x_ref, wq_hbm, wk_hbm, wv_hbm, wo_hbm, o_hbm,
    in_s, w_s, flat_s, x_s, q_s, k_s, v_s, h_s, bad_s, w_sem, out_sem, *, members,
):
    parts = x_ref.shape[0]
    groups = parts // members
    seq = 2 * groups
    rows = parts * 2 * PER
    block = members * 2 * PER
    stride = flat_s.shape[1] // groups
    share = parts // STEPS

    weights_in = []
    for i, w_hbm in enumerate((wq_hbm, wk_hbm, wv_hbm, wo_hbm)):
        weights_in.append(pltpu.make_async_copy(w_hbm.at[pl.ds(1, 2)], w_s.at[i], w_sem.at[i]))
    start_all(weights_in)

    def place(member, j, r):
        inside = r * WIDE + j if j < WIDE else 2 * WIDE + r * NARROW + (j - WIDE)
        return member * 2 * PER + inside

    for i in range(STEPS):
        for g in range(i * groups // STEPS, (i + 1) * groups // STEPS):
            wide = x_ref[g * members : (g + 1) * members].astype(f32).reshape(block, D)
            for c in range(2):
                flat_s[c, g * stride : g * stride + block, :] = wide[:, 128 * c : 128 * c + 128]
    for member in range(members):
        for j in range(PER):
            base = (member * PER + j) * seq
            for c in range(2):
                pieces = [flat_s[c, pl.ds(place(member, j, r), groups, stride=stride), :] for r in range(2)]
                x_s[base : base + seq, 128 * c : 128 * c + 128] = jnp.concatenate(pieces, axis=0).astype(bf16)
    for copy in weights_in:
        copy.wait()

    x = x_s[...]
    for b in range(2):
        q_s[b] = (dot(x, w_s[0, b]) * QUERY_FACTOR).astype(bf16)
        k_s[b] = dot(x, w_s[1, b]).astype(bf16)
        v_s[b] = dot(x, w_s[2, b]).astype(bf16)

    own = lax.broadcasted_iota(jnp.int32, (4 * seq, 128), 0) // seq
    own = own == lax.broadcasted_iota(jnp.int32, (4 * seq, 128), 1) // HEAD
    ones = jnp.where(own, 1.0, 0.0).astype(bf16)

    def lat_score(spot, shifted):
        at, lanes = spot
        keys = jnp.concatenate([k_s[0, pl.ds(at, seq), lanes]] * 4, axis=0)
        keys = jnp.where(own, keys, jnp.zeros_like(keys))
        scores = lax.dot_general(q_s[0, pl.ds(at, seq), lanes], keys, NT, preferred_element_type=f32)
        if shifted:
            head = lax.broadcasted_iota(jnp.int32, scores.shape, 1) // seq
            tops = jnp.zeros_like(scores)
            for h in range(4):
                mine = head == h
                top = jnp.max(jnp.where(mine, scores, -jnp.inf), axis=1, keepdims=True)
                tops = jnp.where(mine, top, tops)
            scores = scores - tops
        return scores

    def lat_finish(spot, scores):
        at, lanes = spot
        values = jnp.concatenate([v_s[0, pl.ds(at, seq), lanes]] * 4, axis=0)
        values = jnp.where(own, values, jnp.zeros_like(values))
        weights = jnp.exp2(scores).astype(bf16)
        return dot(weights, values), dot(weights, ones)

    def lat_attend(shifted, several):
        @pl.loop(0, members * PER // several)
        def _(n):
            spots = [
                (pl.multiple_of((n * several + u) * seq, seq), slice(128 * c, 128 * c + 128))
                for u in range(several)
                for c in range(2)
            ]
            scores = [lat_score(spot, shifted) for spot in spots]
            results = [lat_finish(spot, score) for spot, score in zip(spots, scores)]
            for (at, lanes), (mixed, total) in zip(spots, results):
                h_s[pl.ds(at, seq), lanes] = (mixed / total).astype(bf16)
            if not shifted:
                bad_s[...] = functools.reduce(jnp.maximum, [out_of_range(total) for _, total in results], bad_s[...])

    bad_s[...] = jnp.zeros_like(bad_s)
    lat_attend(False, 16)
    bad = jnp.max(bad_s[...])

    @pl.when(bad > 0.0)
    def _():
        lat_attend(True, 1)

    last = members - 1
    count = PER * seq
    piece = count // 4
    feature = lax.broadcasted_iota(jnp.int32, (D, 128), 0) // HEAD
    lane = lax.broadcasted_iota(jnp.int32, (D, 128), 1)
    fold = jnp.concatenate(
        [
            jnp.where(lane == n * 32 + m * HEADS + feature, 1.0, 0.0).astype(bf16)
            for m in range(members)
            for n in range(last)
        ],
        axis=0,
    )
    slot = lax.broadcasted_iota(jnp.int32, (128, D), 0)
    feature = lax.broadcasted_iota(jnp.int32, (128, D), 1) // HEAD
    spread = [
        jnp.concatenate(
            [jnp.where(slot == n * 32 + m * HEADS + feature, 1.0, 0.0).astype(bf16) for n in range(last)], axis=1
        )
        for m in range(members)
    ]
    spots = [[i * piece + member * count for member in range(members)] for i in range(4)]

    def over_members(combine, x):
        return functools.reduce(combine, [pltpu.roll(x, 32 * n, 1) for n in (1, 2, 3)], x)

    def mem_weights(ats):
        keys = [k_s[1, at : at + piece, :].astype(f32) for at in ats]
        keys = [key - keys[last] for key in keys[:last]]
        queries = [q_s[1, at : at + piece, :].astype(f32) for at in ats]
        scores = dot(jnp.concatenate([(query * key).astype(bf16) for query in queries for key in keys], axis=1), fold)
        weights = jnp.exp2(scores - over_members(jnp.maximum, scores))
        return (weights / over_members(jnp.add, weights)).astype(bf16)

    def mem_finish(ats, weights):
        values = [v_s[1, at : at + piece, :].astype(f32) for at in ats]
        base_value = values[last]
        values = [value - base_value for value in values[:last]]
        for m in range(members):
            wide = dot(weights, spread[m])
            terms = [wide[:, n * D : n * D + D] * values[n] for n in range(last)]
            h_s[ats[m] : ats[m] + piece, D : 2 * D] = functools.reduce(jnp.add, terms, base_value).astype(bf16)

    ahead = mem_weights(spots[0])
    for i, ats in enumerate(spots):
        weights = ahead
        if i + 1 < len(spots):
            ahead = mem_weights(spots[i + 1])
        mem_finish(ats, weights)

    for member in range(members):
        base = member * PER * seq
        h = h_s[base : base + PER * seq, :]
        out = dot(h[:, 0:D], w_s[3, 0]) + dot(h[:, D : 2 * D], w_s[3, 1])
        for j in range(PER):
            for c in range(2):
                for r in range(2):
                    at = j * seq + r * groups
                    value = out[at : at + groups, 128 * c : 128 * c + 128]
                    flat_s[c, pl.ds(place(member, j, r), groups, stride=stride), :] = value
    stores = []
    for i in range(STEPS):
        for g in range(i * groups // STEPS, (i + 1) * groups // STEPS):
            both = jnp.concatenate([flat_s[c, g * stride : g * stride + block, :] for c in range(2)], axis=1)
            in_s[g * members : (g + 1) * members] = both.reshape(members, 2 * PER, D).astype(bf16)
        part = pl.ds(i * share, share)
        stores.append(pltpu.make_async_copy(in_s.at[part], o_hbm.at[part], out_sem.at[i]))
        stores[-1].start()
    for copy in stores:
        copy.wait()


def cross(received, w_query, w_key, w_value, w_out, members):
    parts = received.shape[0]
    rows = parts * 2 * PER
    groups = parts // members
    return pl.pallas_call(
        functools.partial(cross_kernel, members=members),
        out_shape=jax.ShapeDtypeStruct(received.shape, bf16),
        in_specs=[pl.BlockSpec(memory_space=pltpu.VMEM)] + [ANY] * 4,
        out_specs=ANY,
        scratch_shapes=[
            pltpu.VMEM(received.shape, bf16),
            pltpu.VMEM((4, 2, D, D), bf16),
            pltpu.VMEM((2, rows + 8 * groups, 128), f32),
            pltpu.VMEM((rows, D), bf16),
            pltpu.VMEM((2, rows, D), bf16),
            pltpu.VMEM((2, rows, D), bf16),
            pltpu.VMEM((2, rows, D), bf16),
            pltpu.VMEM((rows, 2 * D), bf16),
            pltpu.VMEM((2 * groups, 128), f32),
            pltpu.SemaphoreType.DMA((4,)),
            pltpu.SemaphoreType.DMA((STEPS,)),
        ],
        compiler_params=pltpu.CompilerParams(vmem_limit_bytes=40 * MIB),
        cost_estimate=pl.CostEstimate(flops=12_000_000_000, bytes_accessed=5_000_000, transcendentals=0),
        name="cross",
    )(received, w_query, w_key, w_value, w_out)


def on_device(fields, norm_gain, w_query, w_key, w_value, w_out, *, lat, members):
    state = fields.reshape(fields.shape[1:])
    gain = norm_gain.reshape(1, D)
    axes = ("lat", "mem")
    weights = (w_query, w_key, w_value, w_out)
    packed = pack(state, gain, lat * members)
    received = lax.all_to_all(packed, axes, split_axis=0, concat_axis=0, tiled=True)
    partial = lon_row(packed, state, gain, *weights, 0)
    sent = cross(received, *weights, members)
    returned = lax.all_to_all(sent, axes, split_axis=0, concat_axis=0, tiled=True)
    partial = lon_row(sent, state, gain, *weights, 1, (partial,))
    return unpack(partial, returned).reshape(fields.shape)


def solution(mesh):
    return jax.shard_map(
        functools.partial(on_device, lat=mesh.shape["lat"], members=mesh.shape["mem"]),
        mesh=mesh,
        in_specs=(P("mem", "lat", None, None), P(), P(), P(), P(), P()),
        out_specs=P("mem", "lat", None, None),
        check_vma=False,
    )
```

```python
import functools
import math

import jax
import jax.numpy as jnp
from jax import lax
from jax.experimental import pallas as pl
from jax.experimental.pallas import tpu as pltpu
from jax.sharding import PartitionSpec as P

HEADS = 8
HEAD = 32
D = 256
EPSILON = 1e-06
QUERY_FACTOR = math.log2(math.e) / math.sqrt(HEAD)
LOW, HIGH = 2.0**-100, 2.0**120
NT = (((1,), (1,)), ((), ()))
MIB = 2**20
WIDE, NARROW = 8, 4
PER = WIDE + NARROW
STEPS = 4

f32, bf16 = jnp.float32, jnp.bfloat16


def rms_normed(fields, gain):
    wide = fields.astype(f32)
    meansq = jnp.mean(wide * wide, axis=-1, keepdims=True)
    return wide * lax.rsqrt(meansq + EPSILON) * gain


def dot(a, b):
    return jnp.dot(a, b, preferred_element_type=f32)


ANY = pl.BlockSpec(memory_space=pl.ANY)


def start_all(copies):
    for copy in copies:
        copy.start()
    return copies


def pieces(parts, lon):
    cut = parts * WIDE
    return [(cut, lon - cut)] + [(cut // STEPS * i, cut // STEPS) for i in range(STEPS)]


def halves_swapped(a, b):
    upper = lax.broadcasted_iota(jnp.int32, a.shape, 1) < 4
    return jnp.where(upper, a, pltpu.roll(b, 4, 1)), jnp.where(upper, pltpu.roll(a, 4, 1), b)


def pack_kernel(f_hbm, g_hbm, o_hbm, f_s, g_s, o_s, sem, g_sem, o_sem, *, parts):
    lon = f_hbm.shape[1]
    places = pieces(parts, lon)
    g_copy = pltpu.make_async_copy(g_hbm, g_s, g_sem)
    loads = [
        pltpu.make_async_copy(f_hbm.at[:, pl.ds(at, n)], f_s.at[:, pl.ds(at, n)], sem.at[i])
        for i, (at, n) in enumerate(places)
    ]
    start_all([g_copy] + loads)
    g_copy.wait()
    gain = g_s[...]
    stores = []
    for i, (at, n) in enumerate(places):
        loads[i].wait()
        rows = [rms_normed(f_s[r, at : at + n, :], gain).reshape(n // 8, 8, D) for r in range(2)]
        if i == 0:
            have = n // NARROW
            both = jnp.stack(halves_swapped(*rows), axis=1).reshape(have, 8, D)
            o_s[0:have, 16:24, :] = both.astype(bf16)
            o_s[have:parts, 16:24, :] = jnp.zeros((parts - have, 8, D), bf16)
        else:
            part = slice(at // WIDE, (at + n) // WIDE)
            o_s[part, 0:16, :] = jnp.concatenate(rows, axis=1).astype(bf16)
            stores.append(pltpu.make_async_copy(o_s.at[part], o_hbm.at[part], o_sem.at[i - 1]))
            stores[-1].start()
    for copy in stores:
        copy.wait()


def pack(fields, gain, parts):
    return pl.pallas_call(
        functools.partial(pack_kernel, parts=parts),
        out_shape=jax.ShapeDtypeStruct((parts, 2 * PER, D), bf16),
        in_specs=[ANY, ANY],
        out_specs=ANY,
        scratch_shapes=[
            pltpu.VMEM(fields.shape, bf16),
            pltpu.VMEM((1, D), f32),
            pltpu.VMEM((parts, 2 * PER, D), bf16),
            pltpu.SemaphoreType.DMA((STEPS + 1,)),
            pltpu.SemaphoreType.DMA,
            pltpu.SemaphoreType.DMA((STEPS,)),
        ],
        compiler_params=pltpu.CompilerParams(vmem_limit_bytes=60 * MIB),
        cost_estimate=pl.CostEstimate(flops=4_000_000, bytes_accessed=3_000_000, transcendentals=0),
        name="pack",
    )(fields, gain)


def unpack_kernel(p_hbm, x_ref, o_hbm, p_s, in_sem, out_sem):
    parts, lon = x_ref.shape[0], p_hbm.shape[1]
    places = pieces(parts, lon)
    loads = [
        pltpu.make_async_copy(p_hbm.at[:, pl.ds(at, n)], p_s.at[:, pl.ds(at, n)], in_sem.at[i])
        for i, (at, n) in enumerate(places)
    ]
    start_all(loads)
    stores = []
    for i, (at, n) in enumerate(places):
        loads[i].wait()
        if i == 0:
            both = x_ref[0 : n // NARROW, 16:24, :].astype(f32).reshape(n // 8, 2, 8, D)
            add = halves_swapped(both[:, 0], both[:, 1])
        else:
            both = x_ref[at // WIDE : (at + n) // WIDE, 0:16, :].astype(f32)
            add = (both[:, 0:8, :], both[:, 8:16, :])
        for r in range(2):
            p_s[r, at : at + n, :] = (p_s[r, at : at + n, :].astype(f32) + add[r].reshape(n, D)).astype(bf16)
        part = pl.ds(at, n)
        stores.append(pltpu.make_async_copy(p_s.at[:, part], o_hbm.at[:, part], out_sem.at[i]))
        stores[-1].start()
    for copy in stores:
        copy.wait()


def unpack(partial, returned):
    return pl.pallas_call(
        unpack_kernel,
        out_shape=jax.ShapeDtypeStruct(partial.shape, bf16),
        in_specs=[ANY, pl.BlockSpec(memory_space=pltpu.VMEM)],
        out_specs=ANY,
        input_output_aliases={0: 0},
        scratch_shapes=[
            pltpu.VMEM(partial.shape, bf16),
            pltpu.SemaphoreType.DMA((STEPS + 1,)),
            pltpu.SemaphoreType.DMA((STEPS + 1,)),
        ],
        compiler_params=pltpu.CompilerParams(vmem_limit_bytes=40 * MIB),
        cost_estimate=pl.CostEstimate(flops=4_000_000, bytes_accessed=6_000_000, transcendentals=0),
        name="unpack",
    )(partial, returned)


def out_of_range(total):
    return jnp.where((total > LOW) & (total < HIGH), 0.0, 1.0)


def lon_kernel(after, f_hbm, g_hbm, wq_hbm, wk_hbm, wv_hbm, wo_hbm, *refs, row_at):
    o_hbm, f_s, g_s, w_s, x_s, q_s, kt_s, v_s, kb_s, vb_s, acc_s, o_s, f_sem, w_sem, o_sem = refs[-15:]
    del after
    lon = f_s.shape[0]
    main = lon // 256 * 256
    rest = lon - main
    thirds = [slice(lon // 3 * i, lon // 3 * (i + 1)) for i in range(3)]
    g_copy = pltpu.make_async_copy(g_hbm, g_s, f_sem.at[3])
    f_copies = [pltpu.make_async_copy(f_hbm.at[row_at, at], f_s.at[at], f_sem.at[i]) for i, at in enumerate(thirds)]
    w_copies = [
        pltpu.make_async_copy(w_hbm.at[0], w_s.at[i], w_sem.at[i])
        for i, w_hbm in enumerate((wk_hbm, wq_hbm, wv_hbm, wo_hbm))
    ]
    start_all([g_copy] + f_copies + w_copies)
    g_copy.wait()
    for i, at in enumerate(thirds):
        f_copies[i].wait()
        x_s[at, :] = rms_normed(f_s[at, :], g_s[...]).astype(bf16)
    w_copies[0].wait()
    kt_s[...] = lax.dot_general(w_s[0].T, x_s[...], NT, preferred_element_type=f32).astype(bf16)
    w_copies[1].wait()
    q_s[...] = (dot(x_s[...], w_s[1]) * QUERY_FACTOR).astype(bf16)
    w_copies[2].wait()
    v_s[...] = dot(x_s[...], w_s[2]).astype(bf16)
    w_copies[3].wait()
    key_rest = dot(x_s[main:lon, :], w_s[0]).astype(bf16)
    value_rest = v_s[main:lon, :]
    lane_rest = lax.broadcasted_iota(jnp.int32, (rest, D), 1) // HEAD
    for head in range(HEADS):
        own = lane_rest == head
        half, slot = head // 4, head % 4
        kb_s[head * rest : (head + 1) * rest, :] = jnp.where(own, key_rest, jnp.zeros_like(key_rest))
        mine = slice(128 * half, 128 * half + 128)
        values = jnp.where(own, value_rest, jnp.zeros_like(value_rest))[:, mine]
        ones = jnp.where(own, 1.0, 0.0).astype(bf16)[:, mine]
        vb_s[half, slot * rest : (slot + 1) * rest, :] = jnp.concatenate([values, ones], axis=1)
    row = lax.broadcasted_iota(jnp.int32, (128, lon), 0) // HEAD
    lane = lax.broadcasted_iota(jnp.int32, (lon, 128), 1) // HEAD
    block = lon // 2

    def attend(shifted):
        keyed = lon if shifted else main
        acc_s[...] = jnp.zeros_like(acc_s)

        @pl.loop(0, HEADS)
        def _(head):
            half = head // 4
            at = pl.multiple_of(half * 128, 128)
            keys = kt_s[pl.ds(at, 128), 0:keyed]
            keys = jnp.where(row[:, 0:keyed] == head % 4, keys, jnp.zeros_like(keys))
            own = lane[0:keyed] == head % 4
            values = v_s[0:keyed, pl.ds(at, 128)]
            ones = jnp.where(own, 1.0, 0.0).astype(bf16)
            values = jnp.concatenate([jnp.where(own, values, jnp.zeros_like(values)), ones], axis=1)

            def score(start):
                scores = dot(q_s[start : start + block, pl.ds(at, 128)], keys)
                if shifted:
                    scores = scores - jnp.max(scores, axis=1, keepdims=True)
                return scores

            ahead = score(0)
            for start in range(0, lon, block):
                weights = jnp.exp2(ahead).astype(bf16)
                if start + block < lon:
                    ahead = score(start + block)
                acc_s[half, start : start + block, :] += dot(weights, values)

    attend(False)

    def score_rest(at):
        return lax.dot_general(q_s[at, :], kb_s[...], NT, preferred_element_type=f32)

    ahead = score_rest(thirds[0])
    for i, at in enumerate(thirds):
        weights = jnp.exp2(ahead).astype(bf16)
        if i + 1 < len(thirds):
            ahead = score_rest(thirds[i + 1])
        for half in range(2):
            acc_s[half, at, :] += dot(weights[:, 4 * rest * half : 4 * rest * (half + 1)], vb_s[half])
    bad = jnp.max(out_of_range(acc_s[:, :, 128:256]))

    @pl.when(bad > 0.0)
    def _():
        attend(True)

    stores = []
    for i, at in enumerate(thirds):
        heads = [(acc_s[c, at, 0:128] / acc_s[c, at, 128:256]).astype(bf16) for c in range(2)]
        o_s[at, :] = (f_s[at, :].astype(f32) + dot(jnp.concatenate(heads, axis=1), w_s[3])).astype(bf16)
        stores.append(pltpu.make_async_copy(o_s.at[at], o_hbm.at[row_at, at], o_sem.at[i]))
        stores[-1].start()
    for copy in stores:
        copy.wait()


def lon_row(after, fields, gain, w_query, w_key, w_value, w_out, row_at, other=()):
    lon = fields.shape[1]
    rest = lon % 256
    return pl.pallas_call(
        functools.partial(lon_kernel, row_at=row_at),
        out_shape=jax.ShapeDtypeStruct(fields.shape, bf16),
        in_specs=[ANY] * (7 + len(other)),
        out_specs=ANY,
        input_output_aliases={7: 0} if other else {},
        scratch_shapes=[
            pltpu.VMEM((lon, D), bf16),
            pltpu.VMEM((1, D), f32),
            pltpu.VMEM((4, D, D), bf16),
            pltpu.VMEM((lon, D), bf16),
            pltpu.VMEM((lon, D), bf16),
            pltpu.VMEM((D, lon), bf16),
            pltpu.VMEM((lon, D), bf16),
            pltpu.VMEM((HEADS * rest, D), bf16),
            pltpu.VMEM((2, HEADS // 2 * rest, D), bf16),
            pltpu.VMEM((2, lon, D), f32),
            pltpu.VMEM((lon, D), bf16),
            pltpu.SemaphoreType.DMA((4,)),
            pltpu.SemaphoreType.DMA((4,)),
            pltpu.SemaphoreType.DMA((3,)),
        ],
        compiler_params=pltpu.CompilerParams(vmem_limit_bytes=60 * MIB),
        cost_estimate=pl.CostEstimate(flops=25_000_000_000, bytes_accessed=3_000_000, transcendentals=0),
        name="lon",
    )(after, fields, gain, w_query, w_key, w_value, w_out, *other)


def cross_kernel(
    x_ref, wq_hbm, wk_hbm, wv_hbm, wo_hbm, o_hbm,
    in_s, w_s, flat_s, x_s, q_s, k_s, v_s, h_s, bad_s, w_sem, out_sem, *, members,
):
    parts = x_ref.shape[0]
    groups = parts // members
    seq = 2 * groups
    rows = parts * 2 * PER
    block = members * 2 * PER
    stride = flat_s.shape[1] // groups
    share = parts // STEPS

    weights_in = []
    for i, w_hbm in enumerate((wq_hbm, wk_hbm, wv_hbm, wo_hbm)):
        weights_in.append(pltpu.make_async_copy(w_hbm.at[pl.ds(1, 2)], w_s.at[i], w_sem.at[i]))
    start_all(weights_in)

    def place(member, j, r):
        inside = r * WIDE + j if j < WIDE else 2 * WIDE + r * NARROW + (j - WIDE)
        return member * 2 * PER + inside

    for i in range(STEPS):
        for g in range(i * groups // STEPS, (i + 1) * groups // STEPS):
            wide = x_ref[g * members : (g + 1) * members].astype(f32).reshape(block, D)
            for c in range(2):
                flat_s[c, g * stride : g * stride + block, :] = wide[:, 128 * c : 128 * c + 128]
    for member in range(members):
        for j in range(PER):
            base = (member * PER + j) * seq
            for c in range(2):
                pieces = [flat_s[c, pl.ds(place(member, j, r), groups, stride=stride), :] for r in range(2)]
                x_s[base : base + seq, 128 * c : 128 * c + 128] = jnp.concatenate(pieces, axis=0).astype(bf16)
    for copy in weights_in:
        copy.wait()

    x = x_s[...]
    for b in range(2):
        q_s[b] = (dot(x, w_s[0, b]) * QUERY_FACTOR).astype(bf16)
        k_s[b] = dot(x, w_s[1, b]).astype(bf16)
        v_s[b] = dot(x, w_s[2, b]).astype(bf16)

    own = lax.broadcasted_iota(jnp.int32, (4 * seq, 128), 0) // seq
    own = own == lax.broadcasted_iota(jnp.int32, (4 * seq, 128), 1) // HEAD
    ones = jnp.where(own, 1.0, 0.0).astype(bf16)

    def lat_score(spot, shifted):
        at, lanes = spot
        keys = jnp.concatenate([k_s[0, pl.ds(at, seq), lanes]] * 4, axis=0)
        keys = jnp.where(own, keys, jnp.zeros_like(keys))
        scores = lax.dot_general(q_s[0, pl.ds(at, seq), lanes], keys, NT, preferred_element_type=f32)
        if shifted:
            head = lax.broadcasted_iota(jnp.int32, scores.shape, 1) // seq
            tops = jnp.zeros_like(scores)
            for h in range(4):
                mine = head == h
                top = jnp.max(jnp.where(mine, scores, -jnp.inf), axis=1, keepdims=True)
                tops = jnp.where(mine, top, tops)
            scores = scores - tops
        return scores

    def lat_finish(spot, scores):
        at, lanes = spot
        values = jnp.concatenate([v_s[0, pl.ds(at, seq), lanes]] * 4, axis=0)
        values = jnp.where(own, values, jnp.zeros_like(values))
        weights = jnp.exp2(scores).astype(bf16)
        return dot(weights, values), dot(weights, ones)

    def lat_attend(shifted, several):
        @pl.loop(0, members * PER // several)
        def _(n):
            spots = [
                (pl.multiple_of((n * several + u) * seq, seq), slice(128 * c, 128 * c + 128))
                for u in range(several)
                for c in range(2)
            ]
            scores = [lat_score(spot, shifted) for spot in spots]
            results = [lat_finish(spot, score) for spot, score in zip(spots, scores)]
            for (at, lanes), (mixed, total) in zip(spots, results):
                h_s[pl.ds(at, seq), lanes] = (mixed / total).astype(bf16)
            if not shifted:
                bad_s[...] = functools.reduce(jnp.maximum, [out_of_range(total) for _, total in results], bad_s[...])

    bad_s[...] = jnp.zeros_like(bad_s)
    lat_attend(False, 16)
    bad = jnp.max(bad_s[...])

    @pl.when(bad > 0.0)
    def _():
        lat_attend(True, 1)

    last = members - 1
    count = PER * seq
    piece = count // 4
    feature = lax.broadcasted_iota(jnp.int32, (D, 128), 0) // HEAD
    lane = lax.broadcasted_iota(jnp.int32, (D, 128), 1)
    fold = jnp.concatenate(
        [
            jnp.where(lane == n * 32 + m * HEADS + feature, 1.0, 0.0).astype(bf16)
            for m in range(members)
            for n in range(last)
        ],
        axis=0,
    )
    slot = lax.broadcasted_iota(jnp.int32, (128, D), 0)
    feature = lax.broadcasted_iota(jnp.int32, (128, D), 1) // HEAD
    spread = [
        jnp.concatenate(
            [jnp.where(slot == n * 32 + m * HEADS + feature, 1.0, 0.0).astype(bf16) for n in range(last)], axis=1
        )
        for m in range(members)
    ]
    spots = [[i * piece + member * count for member in range(members)] for i in range(4)]

    def over_members(combine, x):
        return functools.reduce(combine, [pltpu.roll(x, 32 * n, 1) for n in (1, 2, 3)], x)

    def mem_weights(ats):
        keys = [k_s[1, at : at + piece, :].astype(f32) for at in ats]
        keys = [key - keys[last] for key in keys[:last]]
        queries = [q_s[1, at : at + piece, :].astype(f32) for at in ats]
        scores = dot(jnp.concatenate([(query * key).astype(bf16) for query in queries for key in keys], axis=1), fold)
        weights = jnp.exp2(scores - over_members(jnp.maximum, scores))
        return (weights / over_members(jnp.add, weights)).astype(bf16)

    def mem_finish(ats, weights):
        values = [v_s[1, at : at + piece, :].astype(f32) for at in ats]
        base_value = values[last]
        values = [value - base_value for value in values[:last]]
        for m in range(members):
            wide = dot(weights, spread[m])
            terms = [wide[:, n * D : n * D + D] * values[n] for n in range(last)]
            h_s[ats[m] : ats[m] + piece, D : 2 * D] = functools.reduce(jnp.add, terms, base_value).astype(bf16)

    ahead = mem_weights(spots[0])
    for i, ats in enumerate(spots):
        weights = ahead
        if i + 1 < len(spots):
            ahead = mem_weights(spots[i + 1])
        mem_finish(ats, weights)

    for member in range(members):
        base = member * PER * seq
        h = h_s[base : base + PER * seq, :]
        out = dot(h[:, 0:D], w_s[3, 0]) + dot(h[:, D : 2 * D], w_s[3, 1])
        for j in range(PER):
            for c in range(2):
                for r in range(2):
                    at = j * seq + r * groups
                    value = out[at : at + groups, 128 * c : 128 * c + 128]
                    flat_s[c, pl.ds(place(member, j, r), groups, stride=stride), :] = value
    stores = []
    for i in range(STEPS):
        for g in range(i * groups // STEPS, (i + 1) * groups // STEPS):
            both = jnp.concatenate([flat_s[c, g * stride : g * stride + block, :] for c in range(2)], axis=1)
            in_s[g * members : (g + 1) * members] = both.reshape(members, 2 * PER, D).astype(bf16)
        part = pl.ds(i * share, share)
        stores.append(pltpu.make_async_copy(in_s.at[part], o_hbm.at[part], out_sem.at[i]))
        stores[-1].start()
    for copy in stores:
        copy.wait()


def cross(received, w_query, w_key, w_value, w_out, members):
    parts = received.shape[0]
    rows = parts * 2 * PER
    groups = parts // members
    return pl.pallas_call(
        functools.partial(cross_kernel, members=members),
        out_shape=jax.ShapeDtypeStruct(received.shape, bf16),
        in_specs=[pl.BlockSpec(memory_space=pltpu.VMEM)] + [ANY] * 4,
        out_specs=ANY,
        scratch_shapes=[
            pltpu.VMEM(received.shape, bf16),
            pltpu.VMEM((4, 2, D, D), bf16),
            pltpu.VMEM((2, rows + 8 * groups, 128), f32),
            pltpu.VMEM((rows, D), bf16),
            pltpu.VMEM((2, rows, D), bf16),
            pltpu.VMEM((2, rows, D), bf16),
            pltpu.VMEM((2, rows, D), bf16),
            pltpu.VMEM((rows, 2 * D), bf16),
            pltpu.VMEM((2 * groups, 128), f32),
            pltpu.SemaphoreType.DMA((4,)),
            pltpu.SemaphoreType.DMA((STEPS,)),
        ],
        compiler_params=pltpu.CompilerParams(vmem_limit_bytes=40 * MIB),
        cost_estimate=pl.CostEstimate(flops=12_000_000_000, bytes_accessed=5_000_000, transcendentals=0),
        name="cross",
    )(received, w_query, w_key, w_value, w_out)


def on_device(fields, norm_gain, w_query, w_key, w_value, w_out, *, lat, members):
    state = fields.reshape(fields.shape[1:])
    gain = norm_gain.reshape(1, D)
    axes = ("lat", "mem")
    weights = (w_query, w_key, w_value, w_out)
    packed = pack(state, gain, lat * members)
    received = lax.all_to_all(packed, axes, split_axis=0, concat_axis=0, tiled=True)
    partial = lon_row(packed, state, gain, *weights, 0)
    sent = cross(received, *weights, members)
    returned = lax.all_to_all(sent, axes, split_axis=0, concat_axis=0, tiled=True)
    partial = lon_row(sent, state, gain, *weights, 1, (partial,))
    return unpack(partial, returned).reshape(fields.shape)


def solution(mesh):
    return jax.shard_map(
        functools.partial(on_device, lat=mesh.shape["lat"], members=mesh.shape["mem"]),
        mesh=mesh,
        in_specs=(P("mem", "lat", None, None), P(), P(), P(), P(), P()),
        out_specs=P("mem", "lat", None, None),
        check_vma=False,
    )
```

```python
import functools
import math

import jax
import jax.numpy as jnp
from jax import lax
from jax.experimental import pallas as pl
from jax.experimental.pallas import tpu as pltpu
from jax.sharding import PartitionSpec as P

HEADS = 8
HEAD = 32
D = 256
EPSILON = 1e-06
QUERY_FACTOR = math.log2(math.e) / math.sqrt(HEAD)
LOW, HIGH = 2.0**-100, 2.0**120
NT = (((1,), (1,)), ((), ()))
MIB = 2**20
WIDE, NARROW = 8, 4
PER = WIDE + NARROW
STEPS = 4

f32, bf16 = jnp.float32, jnp.bfloat16


def rms_normed(fields, gain):
    wide = fields.astype(f32)
    meansq = jnp.mean(wide * wide, axis=-1, keepdims=True)
    return wide * lax.rsqrt(meansq + EPSILON) * gain


def dot(a, b):
    return jnp.dot(a, b, preferred_element_type=f32)


ANY = pl.BlockSpec(memory_space=pl.ANY)


def start_all(copies):
    for copy in copies:
        copy.start()
    return copies


def pieces(parts, lon):
    cut = parts * WIDE
    return [(cut, lon - cut)] + [(cut // STEPS * i, cut // STEPS) for i in range(STEPS)]


def halves_swapped(a, b):
    upper = lax.broadcasted_iota(jnp.int32, a.shape, 1) < 4
    return jnp.where(upper, a, pltpu.roll(b, 4, 1)), jnp.where(upper, pltpu.roll(a, 4, 1), b)


def pack_kernel(f_hbm, g_hbm, o_hbm, f_s, g_s, o_s, sem, g_sem, o_sem, *, parts):
    lon = f_hbm.shape[1]
    places = pieces(parts, lon)
    g_copy = pltpu.make_async_copy(g_hbm, g_s, g_sem)
    loads = [
        pltpu.make_async_copy(f_hbm.at[:, pl.ds(at, n)], f_s.at[:, pl.ds(at, n)], sem.at[i])
        for i, (at, n) in enumerate(places)
    ]
    start_all([g_copy] + loads)
    g_copy.wait()
    gain = g_s[...]
    stores = []
    for i, (at, n) in enumerate(places):
        loads[i].wait()
        rows = [rms_normed(f_s[r, at : at + n, :], gain).reshape(n // 8, 8, D) for r in range(2)]
        if i == 0:
            have = n // NARROW
            both = jnp.stack(halves_swapped(*rows), axis=1).reshape(have, 8, D)
            o_s[0:have, 16:24, :] = both.astype(bf16)
            o_s[have:parts, 16:24, :] = jnp.zeros((parts - have, 8, D), bf16)
        else:
            part = slice(at // WIDE, (at + n) // WIDE)
            o_s[part, 0:16, :] = jnp.concatenate(rows, axis=1).astype(bf16)
            stores.append(pltpu.make_async_copy(o_s.at[part], o_hbm.at[part], o_sem.at[i - 1]))
            stores[-1].start()
    for copy in stores:
        copy.wait()


def pack(fields, gain, parts):
    return pl.pallas_call(
        functools.partial(pack_kernel, parts=parts),
        out_shape=jax.ShapeDtypeStruct((parts, 2 * PER, D), bf16),
        in_specs=[ANY, ANY],
        out_specs=ANY,
        scratch_shapes=[
            pltpu.VMEM(fields.shape, bf16),
            pltpu.VMEM((1, D), f32),
            pltpu.VMEM((parts, 2 * PER, D), bf16),
            pltpu.SemaphoreType.DMA((STEPS + 1,)),
            pltpu.SemaphoreType.DMA,
            pltpu.SemaphoreType.DMA((STEPS,)),
        ],
        compiler_params=pltpu.CompilerParams(vmem_limit_bytes=60 * MIB),
        cost_estimate=pl.CostEstimate(flops=4_000_000, bytes_accessed=3_000_000, transcendentals=0),
        name="pack",
    )(fields, gain)


def unpack_kernel(p_hbm, x_ref, o_hbm, p_s, in_sem, out_sem):
    parts, lon = x_ref.shape[0], p_hbm.shape[1]
    places = pieces(parts, lon)
    loads = [
        pltpu.make_async_copy(p_hbm.at[:, pl.ds(at, n)], p_s.at[:, pl.ds(at, n)], in_sem.at[i])
        for i, (at, n) in enumerate(places)
    ]
    start_all(loads)
    stores = []
    for i, (at, n) in enumerate(places):
        loads[i].wait()
        if i == 0:
            both = x_ref[0 : n // NARROW, 16:24, :].astype(f32).reshape(n // 8, 2, 8, D)
            add = halves_swapped(both[:, 0], both[:, 1])
        else:
            both = x_ref[at // WIDE : (at + n) // WIDE, 0:16, :].astype(f32)
            add = (both[:, 0:8, :], both[:, 8:16, :])
        for r in range(2):
            p_s[r, at : at + n, :] = (p_s[r, at : at + n, :].astype(f32) + add[r].reshape(n, D)).astype(bf16)
        part = pl.ds(at, n)
        stores.append(pltpu.make_async_copy(p_s.at[:, part], o_hbm.at[:, part], out_sem.at[i]))
        stores[-1].start()
    for copy in stores:
        copy.wait()


def unpack(partial, returned):
    return pl.pallas_call(
        unpack_kernel,
        out_shape=jax.ShapeDtypeStruct(partial.shape, bf16),
        in_specs=[ANY, pl.BlockSpec(memory_space=pltpu.VMEM)],
        out_specs=ANY,
        input_output_aliases={0: 0},
        scratch_shapes=[
            pltpu.VMEM(partial.shape, bf16),
            pltpu.SemaphoreType.DMA((STEPS + 1,)),
            pltpu.SemaphoreType.DMA((STEPS + 1,)),
        ],
        compiler_params=pltpu.CompilerParams(vmem_limit_bytes=40 * MIB),
        cost_estimate=pl.CostEstimate(flops=4_000_000, bytes_accessed=6_000_000, transcendentals=0),
        name="unpack",
    )(partial, returned)


def out_of_range(total):
    return jnp.where((total > LOW) & (total < HIGH), 0.0, 1.0)


def lon_kernel(after, f_hbm, g_hbm, wq_hbm, wk_hbm, wv_hbm, wo_hbm, *refs, row_at):
    o_hbm, f_s, g_s, w_s, x_s, q_s, kt_s, v_s, kb_s, vb_s, acc_s, o_s, f_sem, w_sem, o_sem = refs[-15:]
    del after
    lon = f_s.shape[0]
    main = lon // 256 * 256
    rest = lon - main
    thirds = [slice(lon // 3 * i, lon // 3 * (i + 1)) for i in range(3)]
    g_copy = pltpu.make_async_copy(g_hbm, g_s, f_sem.at[3])
    f_copies = [pltpu.make_async_copy(f_hbm.at[row_at, at], f_s.at[at], f_sem.at[i]) for i, at in enumerate(thirds)]
    w_copies = [
        pltpu.make_async_copy(w_hbm.at[0], w_s.at[i], w_sem.at[i])
        for i, w_hbm in enumerate((wk_hbm, wq_hbm, wv_hbm, wo_hbm))
    ]
    start_all([g_copy] + f_copies + w_copies)
    g_copy.wait()
    for i, at in enumerate(thirds):
        f_copies[i].wait()
        x_s[at, :] = rms_normed(f_s[at, :], g_s[...]).astype(bf16)
    w_copies[0].wait()
    kt_s[...] = lax.dot_general(w_s[0].T, x_s[...], NT, preferred_element_type=f32).astype(bf16)
    w_copies[1].wait()
    q_s[...] = (dot(x_s[...], w_s[1]) * QUERY_FACTOR).astype(bf16)
    w_copies[2].wait()
    v_s[...] = dot(x_s[...], w_s[2]).astype(bf16)
    w_copies[3].wait()
    key_rest = dot(x_s[main:lon, :], w_s[0]).astype(bf16)
    value_rest = v_s[main:lon, :]
    lane_rest = lax.broadcasted_iota(jnp.int32, (rest, D), 1) // HEAD
    for head in range(HEADS):
        own = lane_rest == head
        half, slot = head // 4, head % 4
        kb_s[head * rest : (head + 1) * rest, :] = jnp.where(own, key_rest, jnp.zeros_like(key_rest))
        mine = slice(128 * half, 128 * half + 128)
        values = jnp.where(own, value_rest, jnp.zeros_like(value_rest))[:, mine]
        ones = jnp.where(own, 1.0, 0.0).astype(bf16)[:, mine]
        vb_s[half, slot * rest : (slot + 1) * rest, :] = jnp.concatenate([values, ones], axis=1)
    row = lax.broadcasted_iota(jnp.int32, (128, lon), 0) // HEAD
    lane = lax.broadcasted_iota(jnp.int32, (lon, 128), 1) // HEAD
    block = lon // 2

    def attend(shifted):
        keyed = lon if shifted else main
        acc_s[...] = jnp.zeros_like(acc_s)

        @pl.loop(0, HEADS)
        def _(head):
            half = head // 4
            at = pl.multiple_of(half * 128, 128)
            keys = kt_s[pl.ds(at, 128), 0:keyed]
            keys = jnp.where(row[:, 0:keyed] == head % 4, keys, jnp.zeros_like(keys))
            own = lane[0:keyed] == head % 4
            values = v_s[0:keyed, pl.ds(at, 128)]
            ones = jnp.where(own, 1.0, 0.0).astype(bf16)
            values = jnp.concatenate([jnp.where(own, values, jnp.zeros_like(values)), ones], axis=1)

            def score(start):
                scores = dot(q_s[start : start + block, pl.ds(at, 128)], keys)
                if shifted:
                    scores = scores - jnp.max(scores, axis=1, keepdims=True)
                return scores

            ahead = score(0)
            for start in range(0, lon, block):
                weights = jnp.exp2(ahead).astype(bf16)
                if start + block < lon:
                    ahead = score(start + block)
                acc_s[half, start : start + block, :] += dot(weights, values)

    attend(False)

    def score_rest(at):
        return lax.dot_general(q_s[at, :], kb_s[...], NT, preferred_element_type=f32)

    ahead = score_rest(thirds[0])
    for i, at in enumerate(thirds):
        weights = jnp.exp2(ahead).astype(bf16)
        if i + 1 < len(thirds):
            ahead = score_rest(thirds[i + 1])
        for half in range(2):
            acc_s[half, at, :] += dot(weights[:, 4 * rest * half : 4 * rest * (half + 1)], vb_s[half])
    bad = jnp.max(out_of_range(acc_s[:, :, 128:256]))

    @pl.when(bad > 0.0)
    def _():
        attend(True)

    stores = []
    for i, at in enumerate(thirds):
        heads = [(acc_s[c, at, 0:128] / acc_s[c, at, 128:256]).astype(bf16) for c in range(2)]
        o_s[at, :] = (f_s[at, :].astype(f32) + dot(jnp.concatenate(heads, axis=1), w_s[3])).astype(bf16)
        stores.append(pltpu.make_async_copy(o_s.at[at], o_hbm.at[row_at, at], o_sem.at[i]))
        stores[-1].start()
    for copy in stores:
        copy.wait()


def lon_row(after, fields, gain, w_query, w_key, w_value, w_out, row_at, other=()):
    lon = fields.shape[1]
    rest = lon % 256
    return pl.pallas_call(
        functools.partial(lon_kernel, row_at=row_at),
        out_shape=jax.ShapeDtypeStruct(fields.shape, bf16),
        in_specs=[ANY] * (7 + len(other)),
        out_specs=ANY,
        input_output_aliases={7: 0} if other else {},
        scratch_shapes=[
            pltpu.VMEM((lon, D), bf16),
            pltpu.VMEM((1, D), f32),
            pltpu.VMEM((4, D, D), bf16),
            pltpu.VMEM((lon, D), bf16),
            pltpu.VMEM((lon, D), bf16),
            pltpu.VMEM((D, lon), bf16),
            pltpu.VMEM((lon, D), bf16),
            pltpu.VMEM((HEADS * rest, D), bf16),
            pltpu.VMEM((2, HEADS // 2 * rest, D), bf16),
            pltpu.VMEM((2, lon, D), f32),
            pltpu.VMEM((lon, D), bf16),
            pltpu.SemaphoreType.DMA((4,)),
            pltpu.SemaphoreType.DMA((4,)),
            pltpu.SemaphoreType.DMA((3,)),
        ],
        compiler_params=pltpu.CompilerParams(vmem_limit_bytes=60 * MIB),
        cost_estimate=pl.CostEstimate(flops=25_000_000_000, bytes_accessed=3_000_000, transcendentals=0),
        name="lon",
    )(after, fields, gain, w_query, w_key, w_value, w_out, *other)


def cross_kernel(
    x_ref, wq_hbm, wk_hbm, wv_hbm, wo_hbm, o_hbm,
    in_s, w_s, flat_s, x_s, q_s, k_s, v_s, h_s, bad_s, w_sem, out_sem, *, members,
):
    parts = x_ref.shape[0]
    groups = parts // members
    seq = 2 * groups
    rows = parts * 2 * PER
    block = members * 2 * PER
    stride = flat_s.shape[1] // groups
    share = parts // STEPS

    weights_in = []
    for i, w_hbm in enumerate((wq_hbm, wk_hbm, wv_hbm, wo_hbm)):
        weights_in.append(pltpu.make_async_copy(w_hbm.at[pl.ds(1, 2)], w_s.at[i], w_sem.at[i]))
    start_all(weights_in)

    def place(member, j, r):
        inside = r * WIDE + j if j < WIDE else 2 * WIDE + r * NARROW + (j - WIDE)
        return member * 2 * PER + inside

    for i in range(STEPS):
        for g in range(i * groups // STEPS, (i + 1) * groups // STEPS):
            wide = x_ref[g * members : (g + 1) * members].astype(f32).reshape(block, D)
            for c in range(2):
                flat_s[c, g * stride : g * stride + block, :] = wide[:, 128 * c : 128 * c + 128]
    for member in range(members):
        for j in range(PER):
            base = (member * PER + j) * seq
            for c in range(2):
                pieces = [flat_s[c, pl.ds(place(member, j, r), groups, stride=stride), :] for r in range(2)]
                x_s[base : base + seq, 128 * c : 128 * c + 128] = jnp.concatenate(pieces, axis=0).astype(bf16)
    for copy in weights_in:
        copy.wait()

    x = x_s[...]
    for b in range(2):
        q_s[b] = (dot(x, w_s[0, b]) * QUERY_FACTOR).astype(bf16)
        k_s[b] = dot(x, w_s[1, b]).astype(bf16)
        v_s[b] = dot(x, w_s[2, b]).astype(bf16)

    own = lax.broadcasted_iota(jnp.int32, (4 * seq, 128), 0) // seq
    own = own == lax.broadcasted_iota(jnp.int32, (4 * seq, 128), 1) // HEAD
    ones = jnp.where(own, 1.0, 0.0).astype(bf16)

    def lat_score(spot, shifted):
        at, lanes = spot
        keys = jnp.concatenate([k_s[0, pl.ds(at, seq), lanes]] * 4, axis=0)
        keys = jnp.where(own, keys, jnp.zeros_like(keys))
        scores = lax.dot_general(q_s[0, pl.ds(at, seq), lanes], keys, NT, preferred_element_type=f32)
        if shifted:
            head = lax.broadcasted_iota(jnp.int32, scores.shape, 1) // seq
            tops = jnp.zeros_like(scores)
            for h in range(4):
                mine = head == h
                top = jnp.max(jnp.where(mine, scores, -jnp.inf), axis=1, keepdims=True)
                tops = jnp.where(mine, top, tops)
            scores = scores - tops
        return scores

    def lat_finish(spot, scores):
        at, lanes = spot
        values = jnp.concatenate([v_s[0, pl.ds(at, seq), lanes]] * 4, axis=0)
        values = jnp.where(own, values, jnp.zeros_like(values))
        weights = jnp.exp2(scores).astype(bf16)
        return dot(weights, values), dot(weights, ones)

    def lat_attend(shifted, several):
        @pl.loop(0, members * PER // several)
        def _(n):
            spots = [
                (pl.multiple_of((n * several + u) * seq, seq), slice(128 * c, 128 * c + 128))
                for u in range(several)
                for c in range(2)
            ]
            scores = [lat_score(spot, shifted) for spot in spots]
            results = [lat_finish(spot, score) for spot, score in zip(spots, scores)]
            for (at, lanes), (mixed, total) in zip(spots, results):
                h_s[pl.ds(at, seq), lanes] = (mixed / total).astype(bf16)
            if not shifted:
                bad_s[...] = functools.reduce(jnp.maximum, [out_of_range(total) for _, total in results], bad_s[...])

    bad_s[...] = jnp.zeros_like(bad_s)
    lat_attend(False, 24)
    bad = jnp.max(bad_s[...])

    @pl.when(bad > 0.0)
    def _():
        lat_attend(True, 1)

    last = members - 1
    count = PER * seq
    piece = count // 3
    feature = lax.broadcasted_iota(jnp.int32, (D, 128), 0) // HEAD
    lane = lax.broadcasted_iota(jnp.int32, (D, 128), 1)
    fold = jnp.concatenate(
        [
            jnp.where(lane == n * 32 + m * HEADS + feature, 1.0, 0.0).astype(bf16)
            for m in range(members)
            for n in range(last)
        ],
        axis=0,
    )
    slot = lax.broadcasted_iota(jnp.int32, (128, D), 0)
    feature = lax.broadcasted_iota(jnp.int32, (128, D), 1) // HEAD
    spread = [
        jnp.concatenate(
            [jnp.where(slot == n * 32 + m * HEADS + feature, 1.0, 0.0).astype(bf16) for n in range(last)], axis=1
        )
        for m in range(members)
    ]
    spots = [[i * piece + member * count for member in range(members)] for i in range(3)]

    def over_members(combine, x):
        return functools.reduce(combine, [pltpu.roll(x, 32 * n, 1) for n in (1, 2, 3)], x)

    def mem_weights(ats):
        keys = [k_s[1, at : at + piece, :].astype(f32) for at in ats]
        keys = [key - keys[last] for key in keys[:last]]
        queries = [q_s[1, at : at + piece, :].astype(f32) for at in ats]
        scores = dot(jnp.concatenate([(query * key).astype(bf16) for query in queries for key in keys], axis=1), fold)
        weights = jnp.exp2(scores - over_members(jnp.maximum, scores))
        return (weights / over_members(jnp.add, weights)).astype(bf16)

    def mem_finish(ats, weights):
        values = [v_s[1, at : at + piece, :].astype(f32) for at in ats]
        base_value = values[last]
        values = [value - base_value for value in values[:last]]
        for m in range(members):
            wide = dot(weights, spread[m])
            terms = [wide[:, n * D : n * D + D] * values[n] for n in range(last)]
            h_s[ats[m] : ats[m] + piece, D : 2 * D] = functools.reduce(jnp.add, terms, base_value).astype(bf16)

    ahead = mem_weights(spots[0])
    for i, ats in enumerate(spots):
        weights = ahead
        if i + 1 < len(spots):
            ahead = mem_weights(spots[i + 1])
        mem_finish(ats, weights)

    for member in range(members):
        base = member * PER * seq
        h = h_s[base : base + PER * seq, :]
        out = dot(h[:, 0:D], w_s[3, 0]) + dot(h[:, D : 2 * D], w_s[3, 1])
        for j in range(PER):
            for c in range(2):
                for r in range(2):
                    at = j * seq + r * groups
                    value = out[at : at + groups, 128 * c : 128 * c + 128]
                    flat_s[c, pl.ds(place(member, j, r), groups, stride=stride), :] = value
    stores = []
    for i in range(STEPS):
        for g in range(i * groups // STEPS, (i + 1) * groups // STEPS):
            both = jnp.concatenate([flat_s[c, g * stride : g * stride + block, :] for c in range(2)], axis=1)
            in_s[g * members : (g + 1) * members] = both.reshape(members, 2 * PER, D).astype(bf16)
        part = pl.ds(i * share, share)
        stores.append(pltpu.make_async_copy(in_s.at[part], o_hbm.at[part], out_sem.at[i]))
        stores[-1].start()
    for copy in stores:
        copy.wait()


def cross(received, w_query, w_key, w_value, w_out, members):
    parts = received.shape[0]
    rows = parts * 2 * PER
    groups = parts // members
    return pl.pallas_call(
        functools.partial(cross_kernel, members=members),
        out_shape=jax.ShapeDtypeStruct(received.shape, bf16),
        in_specs=[pl.BlockSpec(memory_space=pltpu.VMEM)] + [ANY] * 4,
        out_specs=ANY,
        scratch_shapes=[
            pltpu.VMEM(received.shape, bf16),
            pltpu.VMEM((4, 2, D, D), bf16),
            pltpu.VMEM((2, rows + 8 * groups, 128), f32),
            pltpu.VMEM((rows, D), bf16),
            pltpu.VMEM((2, rows, D), bf16),
            pltpu.VMEM((2, rows, D), bf16),
            pltpu.VMEM((2, rows, D), bf16),
            pltpu.VMEM((rows, 2 * D), bf16),
            pltpu.VMEM((2 * groups, 128), f32),
            pltpu.SemaphoreType.DMA((4,)),
            pltpu.SemaphoreType.DMA((STEPS,)),
        ],
        compiler_params=pltpu.CompilerParams(vmem_limit_bytes=40 * MIB),
        cost_estimate=pl.CostEstimate(flops=12_000_000_000, bytes_accessed=5_000_000, transcendentals=0),
        name="cross",
    )(received, w_query, w_key, w_value, w_out)


def on_device(fields, norm_gain, w_query, w_key, w_value, w_out, *, lat, members):
    state = fields.reshape(fields.shape[1:])
    gain = norm_gain.reshape(1, D)
    axes = ("lat", "mem")
    weights = (w_query, w_key, w_value, w_out)
    packed = pack(state, gain, lat * members)
    received = lax.all_to_all(packed, axes, split_axis=0, concat_axis=0, tiled=True)
    partial = lon_row(packed, state, gain, *weights, 0)
    sent = cross(received, *weights, members)
    returned = lax.all_to_all(sent, axes, split_axis=0, concat_axis=0, tiled=True)
    partial = lon_row(sent, state, gain, *weights, 1, (partial,))
    return unpack(partial, returned).reshape(fields.shape)


def solution(mesh):
    return jax.shard_map(
        functools.partial(on_device, lat=mesh.shape["lat"], members=mesh.shape["mem"]),
        mesh=mesh,
        in_specs=(P("mem", "lat", None, None), P(), P(), P(), P(), P()),
        out_specs=P("mem", "lat", None, None),
        check_vma=False,
    )
```

```python
import functools
import math

import jax
import jax.numpy as jnp
from jax import lax
from jax.experimental import pallas as pl
from jax.experimental.pallas import tpu as pltpu
from jax.sharding import PartitionSpec as P

HEADS = 8
HEAD = 32
D = 256
EPSILON = 1e-06
QUERY_FACTOR = math.log2(math.e) / math.sqrt(HEAD)
LOW, HIGH = 2.0**-100, 2.0**120
NT = (((1,), (1,)), ((), ()))
MIB = 2**20
WIDE, NARROW = 8, 4
PER = WIDE + NARROW
STEPS = 4

f32, bf16 = jnp.float32, jnp.bfloat16


def rms_normed(fields, gain):
    wide = fields.astype(f32)
    meansq = jnp.mean(wide * wide, axis=-1, keepdims=True)
    return wide * lax.rsqrt(meansq + EPSILON) * gain


def dot(a, b):
    return jnp.dot(a, b, preferred_element_type=f32)


ANY = pl.BlockSpec(memory_space=pl.ANY)


def start_all(copies):
    for copy in copies:
        copy.start()
    return copies


def pieces(parts, lon):
    cut = parts * WIDE
    return [(cut, lon - cut)] + [(cut // STEPS * i, cut // STEPS) for i in range(STEPS)]


def halves_swapped(a, b):
    upper = lax.broadcasted_iota(jnp.int32, a.shape, 1) < 4
    return jnp.where(upper, a, pltpu.roll(b, 4, 1)), jnp.where(upper, pltpu.roll(a, 4, 1), b)


def pack_kernel(f_hbm, g_hbm, o_hbm, f_s, g_s, o_s, sem, g_sem, o_sem, *, parts):
    lon = f_hbm.shape[1]
    places = pieces(parts, lon)
    g_copy = pltpu.make_async_copy(g_hbm, g_s, g_sem)
    loads = [
        pltpu.make_async_copy(f_hbm.at[:, pl.ds(at, n)], f_s.at[:, pl.ds(at, n)], sem.at[i])
        for i, (at, n) in enumerate(places)
    ]
    start_all([g_copy] + loads)
    g_copy.wait()
    gain = g_s[...]
    stores = []
    for i, (at, n) in enumerate(places):
        loads[i].wait()
        rows = [rms_normed(f_s[r, at : at + n, :], gain).reshape(n // 8, 8, D) for r in range(2)]
        if i == 0:
            have = n // NARROW
            both = jnp.stack(halves_swapped(*rows), axis=1).reshape(have, 8, D)
            o_s[0:have, 16:24, :] = both.astype(bf16)
            o_s[have:parts, 16:24, :] = jnp.zeros((parts - have, 8, D), bf16)
        else:
            part = slice(at // WIDE, (at + n) // WIDE)
            o_s[part, 0:16, :] = jnp.concatenate(rows, axis=1).astype(bf16)
            stores.append(pltpu.make_async_copy(o_s.at[part], o_hbm.at[part], o_sem.at[i - 1]))
            stores[-1].start()
    for copy in stores:
        copy.wait()


def pack(fields, gain, parts):
    return pl.pallas_call(
        functools.partial(pack_kernel, parts=parts),
        out_shape=jax.ShapeDtypeStruct((parts, 2 * PER, D), bf16),
        in_specs=[ANY, ANY],
        out_specs=ANY,
        scratch_shapes=[
            pltpu.VMEM(fields.shape, bf16),
            pltpu.VMEM((1, D), f32),
            pltpu.VMEM((parts, 2 * PER, D), bf16),
            pltpu.SemaphoreType.DMA((STEPS + 1,)),
            pltpu.SemaphoreType.DMA,
            pltpu.SemaphoreType.DMA((STEPS,)),
        ],
        compiler_params=pltpu.CompilerParams(vmem_limit_bytes=60 * MIB),
        cost_estimate=pl.CostEstimate(flops=4_000_000, bytes_accessed=3_000_000, transcendentals=0),
        name="pack",
    )(fields, gain)


def unpack_kernel(p_hbm, x_ref, o_hbm, p_s, in_sem, out_sem):
    parts, lon = x_ref.shape[0], p_hbm.shape[1]
    places = pieces(parts, lon)
    loads = [
        pltpu.make_async_copy(p_hbm.at[:, pl.ds(at, n)], p_s.at[:, pl.ds(at, n)], in_sem.at[i])
        for i, (at, n) in enumerate(places)
    ]
    start_all(loads)
    stores = []
    for i, (at, n) in enumerate(places):
        loads[i].wait()
        if i == 0:
            both = x_ref[0 : n // NARROW, 16:24, :].astype(f32).reshape(n // 8, 2, 8, D)
            add = halves_swapped(both[:, 0], both[:, 1])
        else:
            both = x_ref[at // WIDE : (at + n) // WIDE, 0:16, :].astype(f32)
            add = (both[:, 0:8, :], both[:, 8:16, :])
        for r in range(2):
            p_s[r, at : at + n, :] = (p_s[r, at : at + n, :].astype(f32) + add[r].reshape(n, D)).astype(bf16)
        part = pl.ds(at, n)
        stores.append(pltpu.make_async_copy(p_s.at[:, part], o_hbm.at[:, part], out_sem.at[i]))
        stores[-1].start()
    for copy in stores:
        copy.wait()


def unpack(partial, returned):
    return pl.pallas_call(
        unpack_kernel,
        out_shape=jax.ShapeDtypeStruct(partial.shape, bf16),
        in_specs=[ANY, pl.BlockSpec(memory_space=pltpu.VMEM)],
        out_specs=ANY,
        input_output_aliases={0: 0},
        scratch_shapes=[
            pltpu.VMEM(partial.shape, bf16),
            pltpu.SemaphoreType.DMA((STEPS + 1,)),
            pltpu.SemaphoreType.DMA((STEPS + 1,)),
        ],
        compiler_params=pltpu.CompilerParams(vmem_limit_bytes=40 * MIB),
        cost_estimate=pl.CostEstimate(flops=4_000_000, bytes_accessed=6_000_000, transcendentals=0),
        name="unpack",
    )(partial, returned)


def out_of_range(total):
    return jnp.where((total > LOW) & (total < HIGH), 0.0, 1.0)


def lon_kernel(after, f_hbm, g_hbm, wq_hbm, wk_hbm, wv_hbm, wo_hbm, *refs, row_at):
    o_hbm, f_s, g_s, w_s, x_s, q_s, kt_s, v_s, kb_s, vb_s, acc_s, o_s, f_sem, w_sem, o_sem = refs[-15:]
    del after
    lon = f_s.shape[0]
    main = lon // 256 * 256
    rest = lon - main
    thirds = [slice(lon // 3 * i, lon // 3 * (i + 1)) for i in range(3)]
    g_copy = pltpu.make_async_copy(g_hbm, g_s, f_sem.at[3])
    f_copies = [pltpu.make_async_copy(f_hbm.at[row_at, at], f_s.at[at], f_sem.at[i]) for i, at in enumerate(thirds)]
    w_copies = [
        pltpu.make_async_copy(w_hbm.at[0], w_s.at[i], w_sem.at[i])
        for i, w_hbm in enumerate((wk_hbm, wq_hbm, wv_hbm, wo_hbm))
    ]
    start_all([g_copy] + f_copies + w_copies)
    g_copy.wait()
    for i, at in enumerate(thirds):
        f_copies[i].wait()
        x_s[at, :] = rms_normed(f_s[at, :], g_s[...]).astype(bf16)
    w_copies[0].wait()
    kt_s[...] = lax.dot_general(w_s[0].T, x_s[...], NT, preferred_element_type=f32).astype(bf16)
    w_copies[1].wait()
    q_s[...] = (dot(x_s[...], w_s[1]) * QUERY_FACTOR).astype(bf16)
    w_copies[2].wait()
    v_s[...] = dot(x_s[...], w_s[2]).astype(bf16)
    w_copies[3].wait()
    key_rest = dot(x_s[main:lon, :], w_s[0]).astype(bf16)
    value_rest = v_s[main:lon, :]
    lane_rest = lax.broadcasted_iota(jnp.int32, (rest, D), 1) // HEAD
    for head in range(HEADS):
        own = lane_rest == head
        half, slot = head // 4, head % 4
        kb_s[head * rest : (head + 1) * rest, :] = jnp.where(own, key_rest, jnp.zeros_like(key_rest))
        mine = slice(128 * half, 128 * half + 128)
        values = jnp.where(own, value_rest, jnp.zeros_like(value_rest))[:, mine]
        ones = jnp.where(own, 1.0, 0.0).astype(bf16)[:, mine]
        vb_s[half, slot * rest : (slot + 1) * rest, :] = jnp.concatenate([values, ones], axis=1)
    row = lax.broadcasted_iota(jnp.int32, (128, lon), 0) // HEAD
    lane = lax.broadcasted_iota(jnp.int32, (lon, 128), 1) // HEAD
    block = lon // 2

    def attend(shifted):
        keyed = lon if shifted else main
        acc_s[...] = jnp.zeros_like(acc_s)

        @pl.loop(0, HEADS)
        def _(head):
            half = head // 4
            at = pl.multiple_of(half * 128, 128)
            keys = kt_s[pl.ds(at, 128), 0:keyed]
            keys = jnp.where(row[:, 0:keyed] == head % 4, keys, jnp.zeros_like(keys))
            own = lane[0:keyed] == head % 4
            values = v_s[0:keyed, pl.ds(at, 128)]
            ones = jnp.where(own, 1.0, 0.0).astype(bf16)
            values = jnp.concatenate([jnp.where(own, values, jnp.zeros_like(values)), ones], axis=1)

            def score(start):
                scores = dot(q_s[start : start + block, pl.ds(at, 128)], keys)
                if shifted:
                    scores = scores - jnp.max(scores, axis=1, keepdims=True)
                return scores

            ahead = score(0)
            for start in range(0, lon, block):
                weights = jnp.exp2(ahead).astype(bf16)
                if start + block < lon:
                    ahead = score(start + block)
                acc_s[half, start : start + block, :] += dot(weights, values)

    attend(False)

    def score_rest(at):
        return lax.dot_general(q_s[at, :], kb_s[...], NT, preferred_element_type=f32)

    ahead = score_rest(thirds[0])
    for i, at in enumerate(thirds):
        weights = jnp.exp2(ahead).astype(bf16)
        if i + 1 < len(thirds):
            ahead = score_rest(thirds[i + 1])
        for half in range(2):
            acc_s[half, at, :] += dot(weights[:, 4 * rest * half : 4 * rest * (half + 1)], vb_s[half])
    bad = jnp.max(out_of_range(acc_s[:, :, 128:256]))

    @pl.when(bad > 0.0)
    def _():
        attend(True)

    stores = []
    for i, at in enumerate(thirds):
        heads = [(acc_s[c, at, 0:128] / acc_s[c, at, 128:256]).astype(bf16) for c in range(2)]
        o_s[at, :] = (f_s[at, :].astype(f32) + dot(jnp.concatenate(heads, axis=1), w_s[3])).astype(bf16)
        stores.append(pltpu.make_async_copy(o_s.at[at], o_hbm.at[row_at, at], o_sem.at[i]))
        stores[-1].start()
    for copy in stores:
        copy.wait()


def lon_row(after, fields, gain, w_query, w_key, w_value, w_out, row_at, other=()):
    lon = fields.shape[1]
    rest = lon % 256
    return pl.pallas_call(
        functools.partial(lon_kernel, row_at=row_at),
        out_shape=jax.ShapeDtypeStruct(fields.shape, bf16),
        in_specs=[ANY] * (7 + len(other)),
        out_specs=ANY,
        input_output_aliases={7: 0} if other else {},
        scratch_shapes=[
            pltpu.VMEM((lon, D), bf16),
            pltpu.VMEM((1, D), f32),
            pltpu.VMEM((4, D, D), bf16),
            pltpu.VMEM((lon, D), bf16),
            pltpu.VMEM((lon, D), bf16),
            pltpu.VMEM((D, lon), bf16),
            pltpu.VMEM((lon, D), bf16),
            pltpu.VMEM((HEADS * rest, D), bf16),
            pltpu.VMEM((2, HEADS // 2 * rest, D), bf16),
            pltpu.VMEM((2, lon, D), f32),
            pltpu.VMEM((lon, D), bf16),
            pltpu.SemaphoreType.DMA((4,)),
            pltpu.SemaphoreType.DMA((4,)),
            pltpu.SemaphoreType.DMA((3,)),
        ],
        compiler_params=pltpu.CompilerParams(vmem_limit_bytes=60 * MIB),
        cost_estimate=pl.CostEstimate(flops=25_000_000_000, bytes_accessed=3_000_000, transcendentals=0),
        name="lon",
    )(after, fields, gain, w_query, w_key, w_value, w_out, *other)


def cross_kernel(
    x_ref, wq_hbm, wk_hbm, wv_hbm, wo_hbm, o_hbm,
    in_s, w_s, flat_s, x_s, q_s, k_s, v_s, h_s, bad_s, w_sem, out_sem, *, members,
):
    parts = x_ref.shape[0]
    groups = parts // members
    seq = 2 * groups
    rows = parts * 2 * PER
    block = members * 2 * PER
    stride = flat_s.shape[1] // groups
    share = parts // STEPS

    weights_in = []
    for i, w_hbm in enumerate((wq_hbm, wk_hbm, wv_hbm, wo_hbm)):
        weights_in.append(pltpu.make_async_copy(w_hbm.at[pl.ds(1, 2)], w_s.at[i], w_sem.at[i]))
    start_all(weights_in)

    def place(member, j, r):
        inside = r * WIDE + j if j < WIDE else 2 * WIDE + r * NARROW + (j - WIDE)
        return member * 2 * PER + inside

    for i in range(STEPS):
        for g in range(i * groups // STEPS, (i + 1) * groups // STEPS):
            wide = x_ref[g * members : (g + 1) * members].astype(f32).reshape(block, D)
            for c in range(2):
                flat_s[c, g * stride : g * stride + block, :] = wide[:, 128 * c : 128 * c + 128]
    for member in range(members):
        for j in range(PER):
            base = (member * PER + j) * seq
            for c in range(2):
                pieces = [flat_s[c, pl.ds(place(member, j, r), groups, stride=stride), :] for r in range(2)]
                x_s[base : base + seq, 128 * c : 128 * c + 128] = jnp.concatenate(pieces, axis=0).astype(bf16)
    for copy in weights_in:
        copy.wait()

    x = x_s[...]
    for b in range(2):
        q_s[b] = (dot(x, w_s[0, b]) * QUERY_FACTOR).astype(bf16)
        k_s[b] = dot(x, w_s[1, b]).astype(bf16)
        v_s[b] = dot(x, w_s[2, b]).astype(bf16)

    own = lax.broadcasted_iota(jnp.int32, (4 * seq, 128), 0) // seq
    own = own == lax.broadcasted_iota(jnp.int32, (4 * seq, 128), 1) // HEAD
    ones = jnp.where(own, 1.0, 0.0).astype(bf16)

    def lat_score(spot, shifted):
        at, lanes = spot
        keys = jnp.concatenate([k_s[0, pl.ds(at, seq), lanes]] * 4, axis=0)
        keys = jnp.where(own, keys, jnp.zeros_like(keys))
        scores = lax.dot_general(q_s[0, pl.ds(at, seq), lanes], keys, NT, preferred_element_type=f32)
        if shifted:
            head = lax.broadcasted_iota(jnp.int32, scores.shape, 1) // seq
            tops = jnp.zeros_like(scores)
            for h in range(4):
                mine = head == h
                top = jnp.max(jnp.where(mine, scores, -jnp.inf), axis=1, keepdims=True)
                tops = jnp.where(mine, top, tops)
            scores = scores - tops
        return scores

    def lat_finish(spot, scores):
        at, lanes = spot
        values = jnp.concatenate([v_s[0, pl.ds(at, seq), lanes]] * 4, axis=0)
        values = jnp.where(own, values, jnp.zeros_like(values))
        weights = jnp.exp2(scores).astype(bf16)
        return dot(weights, values), dot(weights, ones)

    def lat_attend(shifted, several):
        @pl.loop(0, members * PER // several)
        def _(n):
            spots = [
                (pl.multiple_of((n * several + u) * seq, seq), slice(128 * c, 128 * c + 128))
                for u in range(several)
                for c in range(2)
            ]
            scores = [lat_score(spot, shifted) for spot in spots]
            results = [lat_finish(spot, score) for spot, score in zip(spots, scores)]
            for (at, lanes), (mixed, total) in zip(spots, results):
                h_s[pl.ds(at, seq), lanes] = (mixed / total).astype(bf16)
            if not shifted:
                bad_s[...] = functools.reduce(jnp.maximum, [out_of_range(total) for _, total in results], bad_s[...])

    bad_s[...] = jnp.zeros_like(bad_s)
    lat_attend(False, 24)
    bad = jnp.max(bad_s[...])

    @pl.when(bad > 0.0)
    def _():
        lat_attend(True, 1)

    last = members - 1
    count = PER * seq
    piece = count // 3
    feature = lax.broadcasted_iota(jnp.int32, (D, 128), 0) // HEAD
    lane = lax.broadcasted_iota(jnp.int32, (D, 128), 1)
    fold = jnp.concatenate(
        [
            jnp.where(lane == n * 32 + m * HEADS + feature, 1.0, 0.0).astype(bf16)
            for m in range(members)
            for n in range(last)
        ],
        axis=0,
    )
    slot = lax.broadcasted_iota(jnp.int32, (128, D), 0)
    feature = lax.broadcasted_iota(jnp.int32, (128, D), 1) // HEAD
    spread = [
        jnp.concatenate(
            [jnp.where(slot == n * 32 + m * HEADS + feature, 1.0, 0.0).astype(bf16) for n in range(last)], axis=1
        )
        for m in range(members)
    ]
    spots = [[i * piece + member * count for member in range(members)] for i in range(3)]

    def over_members(combine, x):
        return functools.reduce(combine, [pltpu.roll(x, 32 * n, 1) for n in (1, 2, 3)], x)

    def mem_weights(ats):
        keys = [k_s[1, at : at + piece, :].astype(f32) for at in ats]
        keys = [key - keys[last] for key in keys[:last]]
        queries = [q_s[1, at : at + piece, :].astype(f32) for at in ats]
        scores = dot(jnp.concatenate([(query * key).astype(bf16) for query in queries for key in keys], axis=1), fold)
        weights = jnp.exp2(scores - over_members(jnp.maximum, scores))
        return (weights / over_members(jnp.add, weights)).astype(bf16)

    def mem_finish(ats, weights):
        values = [v_s[1, at : at + piece, :].astype(f32) for at in ats]
        base_value = values[last]
        values = [value - base_value for value in values[:last]]
        for m in range(members):
            wide = dot(weights, spread[m])
            terms = [wide[:, n * D : n * D + D] * values[n] for n in range(last)]
            h_s[ats[m] : ats[m] + piece, D : 2 * D] = functools.reduce(jnp.add, terms, base_value).astype(bf16)

    ahead = mem_weights(spots[0])
    for i, ats in enumerate(spots):
        weights = ahead
        if i + 1 < len(spots):
            ahead = mem_weights(spots[i + 1])
        mem_finish(ats, weights)

    for member in range(members):
        base = member * PER * seq
        h = h_s[base : base + PER * seq, :]
        out = dot(h, w_s[3].reshape(2 * D, D))
        for j in range(PER):
            for c in range(2):
                for r in range(2):
                    at = j * seq + r * groups
                    value = out[at : at + groups, 128 * c : 128 * c + 128]
                    flat_s[c, pl.ds(place(member, j, r), groups, stride=stride), :] = value
    stores = []
    for i in range(STEPS):
        for g in range(i * groups // STEPS, (i + 1) * groups // STEPS):
            both = jnp.concatenate([flat_s[c, g * stride : g * stride + block, :] for c in range(2)], axis=1)
            in_s[g * members : (g + 1) * members] = both.reshape(members, 2 * PER, D).astype(bf16)
        part = pl.ds(i * share, share)
        stores.append(pltpu.make_async_copy(in_s.at[part], o_hbm.at[part], out_sem.at[i]))
        stores[-1].start()
    for copy in stores:
        copy.wait()


def cross(received, w_query, w_key, w_value, w_out, members):
    parts = received.shape[0]
    rows = parts * 2 * PER
    groups = parts // members
    return pl.pallas_call(
        functools.partial(cross_kernel, members=members),
        out_shape=jax.ShapeDtypeStruct(received.shape, bf16),
        in_specs=[pl.BlockSpec(memory_space=pltpu.VMEM)] + [ANY] * 4,
        out_specs=ANY,
        scratch_shapes=[
            pltpu.VMEM(received.shape, bf16),
            pltpu.VMEM((4, 2, D, D), bf16),
            pltpu.VMEM((2, rows + 8 * groups, 128), f32),
            pltpu.VMEM((rows, D), bf16),
            pltpu.VMEM((2, rows, D), bf16),
            pltpu.VMEM((2, rows, D), bf16),
            pltpu.VMEM((2, rows, D), bf16),
            pltpu.VMEM((rows, 2 * D), bf16),
            pltpu.VMEM((2 * groups, 128), f32),
            pltpu.SemaphoreType.DMA((4,)),
            pltpu.SemaphoreType.DMA((STEPS,)),
        ],
        compiler_params=pltpu.CompilerParams(vmem_limit_bytes=40 * MIB),
        cost_estimate=pl.CostEstimate(flops=12_000_000_000, bytes_accessed=5_000_000, transcendentals=0),
        name="cross",
    )(received, w_query, w_key, w_value, w_out)


def on_device(fields, norm_gain, w_query, w_key, w_value, w_out, *, lat, members):
    state = fields.reshape(fields.shape[1:])
    gain = norm_gain.reshape(1, D)
    axes = ("lat", "mem")
    weights = (w_query, w_key, w_value, w_out)
    packed = pack(state, gain, lat * members)
    received = lax.all_to_all(packed, axes, split_axis=0, concat_axis=0, tiled=True)
    partial = lon_row(packed, state, gain, *weights, 0)
    sent = cross(received, *weights, members)
    returned = lax.all_to_all(sent, axes, split_axis=0, concat_axis=0, tiled=True)
    partial = lon_row(sent, state, gain, *weights, 1, (partial,))
    return unpack(partial, returned).reshape(fields.shape)


def solution(mesh):
    return jax.shard_map(
        functools.partial(on_device, lat=mesh.shape["lat"], members=mesh.shape["mem"]),
        mesh=mesh,
        in_specs=(P("mem", "lat", None, None), P(), P(), P(), P(), P()),
        out_specs=P("mem", "lat", None, None),
        check_vma=False,
    )
```
